32 devices in a mesh: strata: 8 (over z, x), shard: 4 (over y, core).
Axes of the slice: x: 2, y: 2, z: 4, core: 2. Of those that a mesh axis runs over, the one named last changes fastest.
Arguments:
- user_factors: bfloat16 [32768, 512], P(('strata', 'shard')), may hold values from -1.1953125 to 1.1953125
- item_factors: float32 [4096, 512], P(('strata', 'shard')), may hold values from -1.2 to 1.2
- tile_blocks: int32 [8, 4, 3, 8, 2], P('strata', 'shard'), may hold values from 0 to 7, as said below
- tile_counts: int32 [8, 4, 3], P('strata', 'shard'), may hold values from 1 to 8, as said below
- ratings: bfloat16 [8, 4, 3, 8, 128, 128], P('strata', 'shard'), may hold values from -5 to 5
- mask_words: int32 [8, 4, 3, 8, 16, 128], P('strata', 'shard'), may hold values from 0 to 255
Outputs:
- users_out: bfloat16 [32768, 512], P(('strata', 'shard'))
- items_out: float32 [4096, 512], P(('strata', 'shard'))
The draws below stay inside these ranges and needn't reach their ends.
Inputs may be any that keep to these rules, and one draw needn't show every extreme that they name: `tile_blocks`: entry 0 is a user block below 8, entry 1 an item block below 4; the 8 pairs of one stratum, shard and visit are distinct. `tile_counts`: some stratum, shard and visit has exactly 8 live slots in every draw.
All inputs are finite; a program needn't handle non-finite values.
Results may differ from the reference program's by a relative error of at most 0.0095.
Values may be sent and summed in bfloat16 or wider, within the bound.
No kernel may reach another device: no remote copies, remote signals or barrier semaphores. Data moves between devices by JAX's collectives and lax.ppermute only.
A program may use at most 64 MiB of HBM per device.

```python
import jax
import jax.numpy as jnp
from jax import lax

R = 512
TILE = 128
USER_DEV = 1024
P_SIZE = 512
TILES = 8
VISITS = 3
WORDS = 16
USERS = 32768
ITEMS = 4096
N_STRATA = 8
N_SHARD = 4


def draw_tile_blocks(key, part):
    cells = USER_DEV // TILE * (P_SIZE // TILE)
    scores = jax.random.randint(key, (N_STRATA, N_SHARD, VISITS, cells), 0, 1 << 20) * cells
    scores = scores + jnp.arange(cells, dtype=jnp.int32)
    order = jnp.argsort(scores, axis=-1)[..., :TILES].astype(jnp.int32)
    return jnp.stack([order // (P_SIZE // TILE), order % (P_SIZE // TILE)], axis=-1).astype(jnp.int32)


def draw_tile_counts(key, part):
    first, second = jax.random.split(key)
    counts = jax.random.randint(first, (N_STRATA * N_SHARD * VISITS,), 1, TILES + 1)
    spot = jax.random.randint(second, (), 0, N_STRATA * N_SHARD * VISITS)
    counts = jnp.where(jnp.arange(N_STRATA * N_SHARD * VISITS) == spot, TILES, counts)
    return counts.reshape(N_STRATA, N_SHARD, VISITS).astype(jnp.int32)


def draw_mask_words(key, part):
    return jax.random.randint(key, (N_STRATA, N_SHARD, VISITS, TILES, WORDS, TILE), 0, 256).astype(jnp.int32)


def level_of(rng, dims, cuts, low, largest):
    gain = 1.0
    for axis_at, shards_of in cuts:
        heights = jax.random.uniform(jax.random.fold_in(jax.random.fold_in(rng, 6), axis_at), (shards_of,), jnp.float32, low / len(cuts), largest / len(cuts))
        gain = gain * jnp.repeat(jnp.exp(heights), dims[axis_at] // shards_of).reshape((-1,) + (1,) * (len(dims) - 1 - axis_at))
    return gain


def gaussian(own_key, extent, deviation, most, pieces=(), kind=jnp.bfloat16):
    factor_of = level_of(own_key, extent, pieces, -0.22, 0.18) if pieces else 1.0
    values = jax.random.normal(own_key, extent, jnp.float32) * deviation * factor_of
    return jnp.minimum(jnp.maximum(values, -most), most).astype(kind)


def setup_inputs(seed: int = 0) -> dict:
    keys = jax.random.split(jax.random.key(seed), 7)
    user_factors = gaussian(keys[0], (USERS, R), 0.2, 1.1953125, ((0, 32),))
    item_factors = gaussian(keys[1], (ITEMS, R), 0.2, 1.2, ((0, 32),), jnp.float32)
    tile_blocks = draw_tile_blocks(jax.random.fold_in(keys[6], 71), 0)
    tile_counts = draw_tile_counts(jax.random.fold_in(keys[6], 71), 0)
    ratings = gaussian(keys[4], (N_STRATA, N_SHARD, VISITS, TILES, TILE, TILE), 1.0, 5.0, ((0, 8), (1, 4)))
    mask_words = draw_mask_words(jax.random.fold_in(keys[6], 71), 0)
    return dict(user_factors=user_factors, item_factors=item_factors, tile_blocks=tile_blocks, tile_counts=tile_counts, ratings=ratings, mask_words=mask_words)


step_user = 0.05
step_item = 0.004
shrinkage = 0.05


def unpack_mask(words):
    shifts = jnp.arange(8, dtype=jnp.int32)
    bits = jnp.bitwise_and(jnp.right_shift(words[:, :, None, :], shifts[None, None, :, None]), 1)
    return bits.reshape(words.shape[0], words.shape[1] * 8, words.shape[2]).astype(jnp.float32)


def device_terms(user_part, panel_part, blocks, count, rates, words):
    tile_side = rates.shape[-1]
    width = user_part.shape[1]
    user_blocks = user_part.reshape(-1, tile_side, width)
    item_blocks = panel_part.reshape(-1, tile_side, width)
    user_rows = jnp.take(user_blocks, blocks[:, 0], axis=0).astype(jnp.float32)
    item_rows = jnp.take(item_blocks, blocks[:, 1], axis=0).astype(jnp.float32)
    predicted = jnp.einsum('kur,kir->kui', user_rows, item_rows)
    live = (jnp.arange(blocks.shape[0], dtype=jnp.int32) < count).astype(jnp.float32)
    weights = unpack_mask(words) * live[:, None, None]
    error_tile = (weights * (rates.astype(jnp.float32) - predicted)).astype(jnp.bfloat16).astype(jnp.float32)
    user_terms = jnp.einsum('kui,kir->kur', error_tile, item_rows)
    item_terms = jnp.einsum('kui,kur->kir', error_tile, user_rows)
    user_hot = (blocks[:, 0][:, None] == jnp.arange(user_blocks.shape[0], dtype=jnp.int32)[None, :]).astype(jnp.float32)
    item_hot = (blocks[:, 1][:, None] == jnp.arange(item_blocks.shape[0], dtype=jnp.int32)[None, :]).astype(jnp.float32)
    grad_user = jnp.einsum('kb,kur->bur', user_hot, user_terms).reshape(-1, width)
    grad_item = jnp.einsum('kb,kir->bir', item_hot, item_terms).reshape(-1, width)
    return grad_user, grad_item.astype(jnp.bfloat16)


def reference(user_factors, item_factors, tile_blocks, tile_counts, ratings, mask_words):
    users = user_factors.reshape(N_STRATA, N_SHARD, USER_DEV, R)
    panels = item_factors.reshape(N_STRATA, P_SIZE, R)
    for visit in range(VISITS):
        current = jnp.roll(panels, visit, axis=0)
        panel_low = current.astype(jnp.bfloat16)

        def stratum_terms(packed):
            user_part, panel_part, blocks, counts, rates, words = packed
            grad_user, grad_item = jax.vmap(device_terms, in_axes=(0, None, 0, 0, 0, 0))(
                user_part, panel_part, blocks, counts, rates, words)
            return grad_user, jnp.sum(grad_item.astype(jnp.float32), axis=0)

        grad_users, grad_items = lax.map(stratum_terms, (users, panel_low, tile_blocks[:, :, visit],
                                                         tile_counts[:, :, visit], ratings[:, :, visit],
                                                         mask_words[:, :, visit]))
        factor = users.astype(jnp.float32)
        users = (factor + step_user * (grad_users - shrinkage * factor)).astype(jnp.bfloat16)
        current = current + step_item * (grad_items - shrinkage * current)
        panels = jnp.roll(current, -visit, axis=0)
    return users.reshape(-1, R), jnp.roll(panels, VISITS - 1, axis=0).reshape(-1, R)
```

```python
import functools

import jax
import jax.numpy as jnp
from jax import lax
from jax.experimental import pallas as pl
from jax.experimental.pallas import tpu as pltpu
from jax.sharding import PartitionSpec as P

step_user = 0.05
step_item = 0.004
shrinkage = 0.05

VM = pl.BlockSpec(memory_space=pltpu.VMEM)
SM = pl.BlockSpec(memory_space=pltpu.SMEM)
CORES = 2


def rows_at(index, size):
    return pl.ds(pl.multiple_of(index * size, size), size)


def observed(words):
    count, lanes = words.shape
    shift = lax.broadcasted_iota(jnp.int32, (8, lanes), 0)
    parts = [
        jnp.bitwise_and(jnp.right_shift(jnp.broadcast_to(words[i : i + 1], (8, lanes)), shift), 1)
        for i in range(count)
    ]
    return jnp.concatenate(parts, 0) != 0


def tiles_kernel(visit, chips, place, blocks, counts, users, rates, words, *rest):
    pieces, rest = rest[: CORES * chips], rest[CORES * chips :]
    errors, near, far, panel, total = rest
    side = rates.shape[-1]
    rows = pieces[0].shape[0]
    core, chip = place[0], place[1]
    for k in range(chips):
        origin = lax.rem(chip + chips - k, chips)
        panel[rows_at(CORES * origin + core, rows), :] = pieces[k][...]
        panel[rows_at(CORES * origin + 1 - core, rows), :] = pieces[chips + k][...]
    total[...] = jnp.zeros_like(total)

    def tile(k, carry):
        user = blocks[0, 0, visit, k, 0]
        item = blocks[0, 0, visit, k, 1]
        user_rows = users[rows_at(user, side), :]
        item_rows = panel[rows_at(item, side), :]
        predicted = lax.dot_general(
            user_rows, item_rows, (((1,), (1,)), ((), ())), preferred_element_type=jnp.float32
        )
        seen = observed(words[0, 0, visit, k])
        error = jnp.where(seen, rates[0, 0, visit, k].astype(jnp.float32) - predicted, 0.0)
        error = error.astype(jnp.bfloat16)
        errors[k] = error
        total[rows_at(item, side), :] += lax.dot_general(
            error, user_rows, (((0,), (0,)), ((), ())), preferred_element_type=jnp.float32
        )
        return carry

    lax.fori_loop(0, counts[0, 0, visit], tile, 0)
    for k in range(chips):
        owner = lax.rem(chip + k, chips)
        at = pl.ds(k * rows, rows)
        near[at, :] = total[rows_at(CORES * owner + core, rows), :]
        far[at, :] = total[rows_at(CORES * owner + 1 - core, rows), :].astype(far.dtype)


def users_kernel(visit, chips, place, blocks, counts, users, errors, *rest):
    pieces, (out, panel, total) = rest[: CORES * chips], rest[CORES * chips :]
    side = errors.shape[-1]
    rows = pieces[0].shape[0]
    core, chip = place[0], place[1]
    for k in range(chips):
        origin = lax.rem(chip + chips - k, chips)
        panel[rows_at(CORES * origin + core, rows), :] = pieces[k][...]
        panel[rows_at(CORES * origin + 1 - core, rows), :] = pieces[chips + k][...]
    total[...] = jnp.zeros_like(total)

    def tile(k, carry):
        user = blocks[0, 0, visit, k, 0]
        item = blocks[0, 0, visit, k, 1]
        total[rows_at(user, side), :] += jnp.dot(
            errors[k], panel[rows_at(item, side), :], preferred_element_type=jnp.float32
        )
        return carry

    lax.fori_loop(0, counts[0, 0, visit], tile, 0)
    factor = users[...].astype(jnp.float32)
    out[...] = (factor + step_user * (total[...] - shrinkage * factor)).astype(out.dtype)


def add_kernel(near, far, *outs):
    rows = outs[0].shape[0]
    for k, out in enumerate(outs):
        at = pl.ds(k * rows, rows)
        out[...] = (near[at, :] + far[at, :].astype(jnp.float32)).astype(out.dtype)


def tiles(visit, chips, place, blocks, counts, users, rates, words, pieces):
    slots, side = rates.shape[3], rates.shape[-1]
    rows, width = pieces[0].shape
    whole = CORES * chips * rows
    half = chips * rows
    return pl.pallas_call(
        functools.partial(tiles_kernel, visit, chips),
        name="tiles",
        out_shape=(
            pltpu.VMEM((slots, side, side), jnp.bfloat16),
            pltpu.VMEM((half, width), jnp.float32),
            pltpu.VMEM((half, width), jnp.bfloat16),
        ),
        in_specs=[SM] * 3 + [VM] * (3 + len(pieces)),
        out_specs=(VM,) * 3,
        scratch_shapes=[
            pltpu.VMEM((whole, width), jnp.bfloat16),
            pltpu.VMEM((whole, width), jnp.float32),
        ],
        cost_estimate=pl.CostEstimate(flops=4 * slots * side * side * width, bytes_accessed=8 << 20, transcendentals=0),
    )(place, blocks, counts, users, rates, words, *pieces)


def new_users(visit, last, chips, place, blocks, counts, users, errors, pieces):
    slots, side = errors.shape[0], errors.shape[-1]
    rows, width = pieces[0].shape
    whole = CORES * chips * rows
    return pl.pallas_call(
        functools.partial(users_kernel, visit, chips),
        name="users",
        out_shape=jax.ShapeDtypeStruct(users.shape, users.dtype)
        if last
        else pltpu.VMEM(users.shape, users.dtype),
        in_specs=[SM] * 3 + [VM] * (2 + len(pieces)),
        out_specs=VM,
        scratch_shapes=[
            pltpu.VMEM((whole, width), jnp.bfloat16),
            pltpu.VMEM(users.shape, jnp.float32),
        ],
        cost_estimate=pl.CostEstimate(flops=2 * slots * side * side * width, bytes_accessed=8 << 20, transcendentals=0),
    )(place, blocks, counts, users, errors, *pieces)


def added(chips, near, far):
    rows, width = near.shape[0] // chips, near.shape[1]
    return pl.pallas_call(
        add_kernel,
        name="add",
        out_shape=(pltpu.VMEM((rows, width), jnp.bfloat16),) * chips,
        in_specs=[VM] * 2,
        out_specs=(VM,) * chips,
        cost_estimate=pl.CostEstimate(flops=near.size, bytes_accessed=2 << 20, transcendentals=0),
    )(near, far)


def moved(x, by_strata, by_chip, flip, *, strata, peers):
    pairs = []
    for s in range(strata):
        for h in range(peers):
            chip, core = divmod(h, CORES)
            chip = (chip + by_chip) % (peers // CORES)
            core = 1 - core if flip else core
            pairs.append((s * peers + h, (s + by_strata) % strata * peers + chip * CORES + core))
    return lax.ppermute(x, ("strata", "shard"), pairs)


def shards(user_factors, item_factors, tile_blocks, tile_counts, ratings, mask_words):
    strata, peers = lax.axis_size("strata"), lax.axis_size("shard")
    chips = peers // CORES
    move = functools.partial(moved, strata=strata, peers=peers)
    visits = tile_counts.shape[-1]
    me = lax.axis_index("shard")
    place = jnp.stack([me % CORES, me // CORES]).astype(jnp.int32)
    users = user_factors
    panel = item_factors
    panel_low = panel.astype(jnp.bfloat16)
    for visit in range(visits):
        last = visit + 1 == visits
        mine = [panel_low] + [move(panel_low, 0, k, False) for k in range(1, chips)]
        pieces = mine + [move(x, 0, 0, True) for x in mine]
        if not last:
            panel_next = move(panel_low, 1, 0, False)
        errors, near, far = tiles(
            visit, chips, place, tile_blocks, tile_counts, users, ratings, mask_words, pieces
        )
        sums = added(chips, near, move(far, 0, 0, True))
        users = new_users(visit, last, chips, place, tile_blocks, tile_counts, users, errors, pieces)
        if last:
            parts = sums[:1] + tuple(move(sums[k], 0, k, False) for k in range(1, chips))
            old = panel
        else:
            parts = tuple(move(sums[k], 1, k, False) for k in range(chips))
            old = panel_next.astype(jnp.float32)
        summed = functools.reduce(jnp.add, [x.astype(jnp.float32) for x in parts])
        panel = old + step_item * (summed - shrinkage * old)
        panel_low = panel.astype(jnp.bfloat16)
    return (users, panel)


def solution(mesh):
    placed = (
        P(("strata", "shard"), None),
        P(("strata", "shard"), None),
        P("strata", "shard", None, None, None),
        P("strata", "shard", None),
        P("strata", "shard", None, None, None, None),
        P("strata", "shard", None, None, None, None),
    )
    return jax.shard_map(
        shards,
        mesh=mesh,
        in_specs=placed,
        out_specs=(P(("strata", "shard"), None), P(("strata", "shard"), None)),
        check_vma=False,
    )
```

```python
import functools

import jax
import jax.numpy as jnp
from jax import lax
from jax.experimental import pallas as pl
from jax.experimental.pallas import tpu as pltpu
from jax.sharding import PartitionSpec as P

step_user = 0.05
step_item = 0.004
shrinkage = 0.05

VM = pl.BlockSpec(memory_space=pltpu.VMEM)
SM = pl.BlockSpec(memory_space=pltpu.SMEM)
HB = pl.BlockSpec(memory_space=pltpu.HBM)
CORES = 2
CHUNK = 512


def place_of(close, chip, core, rows):
    return pl.multiple_of((chip if close else CORES * chip + core) * rows, rows)


def multiply(a, b, across, over):
    return lax.dot_general(a, b, (((across,), (over,)), ((), ())), preferred_element_type=jnp.float32)


def observed(words):
    count, lanes = words.shape
    shift = lax.broadcasted_iota(jnp.int32, (8, lanes), 0)
    parts = [
        jnp.bitwise_and(jnp.right_shift(jnp.broadcast_to(words[i : i + 1], (8, lanes)), shift), 1)
        for i in range(count)
    ]
    return jnp.concatenate(parts, 0) != 0


def round_kernel(panel, out):
    out[...] = panel[...].astype(out.dtype)


def stage_kernel(*refs):
    count, sem = (len(refs) - 2) // 2, refs[-1]
    copies = [
        pltpu.make_async_copy(refs[1 + i], refs[1 + count + i], sem.at[i]) for i in range(count)
    ]
    for copy in copies:
        copy.start()
    for copy in copies:
        copy.wait()


def prepare_kernel(visit, rows, close, place, blocks, counts, rates, words, keep, send):
    side = rates.shape[-1]
    core = place[0]
    nothing = jnp.full((side, side), jnp.nan, keep.dtype)
    for at in range(0, keep.shape[0], side):
        for lane in range(0, keep.shape[1], side):
            keep[at : at + side, lane : lane + side] = nothing
            send[at : at + side, lane : lane + side] = nothing

    def tile(k, carry):
        users = pl.ds(pl.multiple_of(blocks[0, 0, visit, 0, k] * side, side), side)
        first = blocks[0, 0, visit, 1, k] * side
        seen = observed(words[0, 0, visit, k])
        known = jnp.where(seen, rates[0, 0, visit, k].astype(jnp.float32), jnp.nan)
        if close:
            piece = lax.div(first, rows)
            at = lax.div(piece, CORES) * rows + lax.rem(first, rows)
            at = pl.ds(pl.multiple_of(at, side), side)
            known = known.astype(keep.dtype)

            @pl.when(lax.rem(piece, CORES) == core)
            def _():
                keep[users, at] = known

            @pl.when(lax.rem(piece, CORES) != core)
            def _():
                send[users, at] = known
        else:
            at = pl.ds(pl.multiple_of(first, side), side)
            piece = lax.div(first + lax.broadcasted_iota(jnp.int32, known.shape, 1), rows)
            mine = lax.rem(piece, CORES) == core
            keep[users, at] = jnp.where(mine, known, jnp.nan).astype(keep.dtype)
            send[users, at] = jnp.where(mine, jnp.nan, known).astype(keep.dtype)
        return carry

    lax.fori_loop(0, counts[0, 0, visit], tile, 0)


def tiles_kernel(first, last, chips, close, place, *refs):
    arrived, refs = refs[:chips], refs[chips:]
    (users, peers, rates, peer_rates), refs = refs[:4], refs[4:]
    (low, errors, peer_errors), refs = refs[:3], refs[3:]
    outs, (panel, total) = refs[:-2], refs[-2:]
    core, chip = place[0], place[1]
    rows = panel.shape[0] // chips
    if first:
        for k in range(chips):
            origin = lax.rem(chip + chips - k, chips)
            at = pl.multiple_of(origin * rows, rows)
            panel[pl.ds(at, rows), :] = arrived[k][...].astype(jnp.float32)
    else:
        now = arrived[0][...].astype(jnp.float32)
        for other in arrived[1:]:
            now = now + step_item * other[...].astype(jnp.float32)
        panel[...] = now
    if close:
        low[...] = panel[...].astype(low.dtype)
    else:
        low[...] = jnp.zeros_like(low)
        for j in range(chips):
            low[pl.ds(place_of(close, j, core, rows), rows), :] = panel[
                j * rows : (j + 1) * rows, :
            ].astype(low.dtype)
    for who, known, error in ((users, rates, errors), (peers, peer_rates, peer_errors)):
        for at in range(0, who.shape[0], CHUNK):
            cut = slice(at, at + CHUNK)
            predicted = multiply(who[cut, :], low[...], 1, 1)
            rating = known[cut, :].astype(jnp.float32)
            error[cut, :] = jnp.where(rating == rating, rating - predicted, 0.0).astype(error.dtype)
    total[...] = multiply(errors[...], users[...], 0, 0)
    total[...] += multiply(peer_errors[...], peers[...], 0, 0)
    if last:
        for k in range(chips):
            owner = lax.rem(chip + k, chips)
            term = total[pl.ds(place_of(close, owner, core, rows), rows), :]
            if k == 0:
                old = panel[pl.ds(pl.multiple_of(owner * rows, rows), rows), :]
                term = old + step_item * (term - shrinkage * old)
            outs[k][...] = term.astype(outs[k].dtype)
    else:
        for j in range(chips):
            cut = slice(j * rows, (j + 1) * rows)
            term = total[pl.ds(place_of(close, j, core, rows), rows), :]
            old = panel[cut, :]
            outs[0][cut, :] = (old + step_item * (term - shrinkage * old)).astype(outs[0].dtype)
            outs[1][cut, :] = term.astype(outs[1].dtype)


def users_kernel(count, *refs):
    (low, other_low), refs = refs[:2], refs[2:]
    for i in range(count):
        users, errors, other_errors = refs[3 * i : 3 * i + 3]
        out = refs[3 * count + i]
        for at in range(0, users.shape[0], CHUNK):
            cut = slice(at, at + CHUNK)
            grad = multiply(errors[cut, :], low[...], 1, 0)
            grad = grad + multiply(other_errors[cut, :], other_low[...], 1, 0)
            factor = users[cut, :].astype(jnp.float32)
            out[cut, :] = (factor + step_user * (grad - shrinkage * factor)).astype(out.dtype)


def final_kernel(count, *refs):
    refs = refs[:count] + refs[count + 1 :]
    total = refs[0][...]
    for other in refs[1:count]:
        total = total + step_item * other[...].astype(jnp.float32)
    refs[count][...] = total


def kernel_call(body, name, ins, outs, flops, scratch=(), extra=()):
    return pl.pallas_call(
        body,
        name=name,
        out_shape=tuple(outs),
        in_specs=[SM if x.dtype == jnp.int32 and x.ndim != 6 else VM for x in ins] + [HB] * len(extra),
        out_specs=(VM,) * len(outs),
        scratch_shapes=list(scratch),
        compiler_params=pltpu.CompilerParams(vmem_limit_bytes=16 << 20),
        cost_estimate=pl.CostEstimate(flops=flops, bytes_accessed=1024, transcendentals=0),
    )(*ins, *[pltpu.with_memory_space_constraint(x, pltpu.HBM) for x in extra])


def moved(x, by_strata, by_chip, flip, *, strata, peers):
    pairs = []
    for s in range(strata):
        for h in range(peers):
            chip, core = divmod(h, CORES)
            chip = (chip + by_chip) % (peers // CORES)
            core = 1 - core if flip else core
            pairs.append((s * peers + h, (s + by_strata) % strata * peers + chip * CORES + core))
    return lax.ppermute(x, ("strata", "shard"), pairs)


def shards(user_factors, item_factors, tile_blocks, tile_counts, ratings, mask_words):
    low_type, full_type = jnp.bfloat16, jnp.float32
    strata, peers = lax.axis_size("strata"), lax.axis_size("shard")
    chips = peers // CORES
    move = functools.partial(moved, strata=strata, peers=peers)
    swap = lambda x: move(x, 0, 0, True)
    visits = tile_counts.shape[-1]
    side = ratings.shape[-1]
    rows, width = item_factors.shape
    count = user_factors.shape[0]
    close = rows % side == 0
    held = (chips if close else peers) * rows
    part = chips * rows
    me = lax.axis_index("shard")
    place = jnp.stack([lax.rem(me, CORES), lax.div(me, CORES)]).astype(jnp.int32)
    blocks = jnp.swapaxes(tile_blocks, 3, 4)

    def prepared(visit):
        keep, send = kernel_call(
            functools.partial(prepare_kernel, visit, rows, close),
            "prepare",
            [place, blocks, tile_counts, rates, words],
            [pltpu.VMEM((count, held), low_type)] * 2,
            1024,
        )
        return keep, swap(send)

    panel_low = item_factors.astype(low_type)
    users, rates, words = kernel_call(
        stage_kernel,
        "stage",
        [panel_low],
        [pltpu.VMEM(x.shape, x.dtype) for x in (user_factors, ratings, mask_words)],
        1024,
        [pltpu.SemaphoreType.DMA((3,))],
        [user_factors, ratings, mask_words],
    )
    arrived = [panel_low] + [move(panel_low, 0, k, False) for k in range(1, chips)]
    other_users = swap(users)
    for visit in range(visits):
        last = visit + 1 == visits
        known, other_known = prepared(visit)
        if last:
            sent = [pltpu.VMEM((rows, width), full_type)]
            sent += [pltpu.VMEM((rows, width), low_type)] * (chips - 1)
        else:
            sent = [pltpu.VMEM((part, width), low_type)] * 2
        low, errors, other_errors, *sent = kernel_call(
            functools.partial(tiles_kernel, visit == 0, last, chips, close),
            "tiles",
            [place, *arrived, users, other_users, known, other_known],
            [pltpu.VMEM((held, width), low_type)] + [pltpu.VMEM((count, held), low_type)] * 2 + sent,
            1024,
            [pltpu.VMEM((part, width), full_type), pltpu.VMEM((held, width), full_type)],
        )
        if last:
            arrived = sent[:1] + [move(sent[k], 0, k, False) for k in range(1, chips)]
        else:
            arrived = [move(sent[min(k, 1)], 1, k, False) for k in range(chips)]
        sets = [low, swap(low), users, errors, swap(other_errors)]
        if not last:
            sets += [other_users, other_errors, swap(errors)]
        kind = jax.ShapeDtypeStruct if last else pltpu.VMEM
        users, *other_users = kernel_call(
            functools.partial(users_kernel, 1 if last else 2),
            "users",
            sets,
            [kind((count, width), low_type)] * (1 if last else 2),
            1024,
        )
        if not last:
            other_users = other_users[0]
    (panel,) = kernel_call(
        functools.partial(final_kernel, chips),
        "final",
        arrived,
        [jax.ShapeDtypeStruct((rows, width), full_type)],
        1024,
        extra=[users],
    )
    return (users, panel)


def solution(mesh):
    placed = (
        P(("strata", "shard"), None),
        P(("strata", "shard"), None),
        P("strata", "shard", None, None, None),
        P("strata", "shard", None),
        P("strata", "shard", None, None, None, None),
        P("strata", "shard", None, None, None, None),
    )
    return jax.shard_map(
        shards,
        mesh=mesh,
        in_specs=placed,
        out_specs=(P(("strata", "shard"), None), P(("strata", "shard"), None)),
        check_vma=False,
    )
```

```python
import functools

import jax
import jax.numpy as jnp
from jax import lax
from jax.experimental import pallas as pl
from jax.experimental.pallas import tpu as pltpu
from jax.sharding import PartitionSpec as P

step_user = 0.05
step_item = 0.004
shrinkage = 0.05

VM = pl.BlockSpec(memory_space=pltpu.VMEM)
SM = pl.BlockSpec(memory_space=pltpu.SMEM)
HB = pl.BlockSpec(memory_space=pltpu.HBM)
CORES = 2
CHUNK = 512
MARK = 1 << 32
LEAD = 0


def place_of(close, chip, core, rows):
    return pl.multiple_of((chip if close else CORES * chip + core) * rows, rows)


def multiply(a, b, across, over):
    return lax.dot_general(a, b, (((across,), (over,)), ((), ())), preferred_element_type=jnp.float32)


def observed(words):
    count, lanes = words.shape
    shift = lax.broadcasted_iota(jnp.int32, (8, lanes), 0)
    parts = [
        jnp.bitwise_and(jnp.right_shift(jnp.broadcast_to(words[i : i + 1], (8, lanes)), shift), 1)
        for i in range(count)
    ]
    return jnp.concatenate(parts, 0) != 0


def prepare_kernel(visit, rows, close, place, *refs):
    for i in range(CORES):
        lay_out(visit, rows, close, place[0], *refs[4 * i : 4 * i + 4], refs[4 * CORES + i])


def lay_out(visit, rows, close, core, blocks, counts, rates, words, keep):
    side = rates.shape[-1]
    nothing = jnp.full((side, side), jnp.nan, keep.dtype)
    for at in range(0, keep.shape[0], side):
        for lane in range(0, keep.shape[1], side):
            keep[at : at + side, lane : lane + side] = nothing

    def tile(k, carry):
        users = pl.ds(pl.multiple_of(blocks[0, 0, visit, 0, k] * side, side), side)
        first = blocks[0, 0, visit, 1, k] * side
        seen = observed(words[0, 0, visit, k])
        known = jnp.where(seen, rates[0, 0, visit, k].astype(jnp.float32), jnp.nan)
        if close:
            piece = lax.div(first, rows)
            at = lax.div(piece, CORES) * rows + lax.rem(first, rows)
            at = pl.ds(pl.multiple_of(at, side), side)
            known = known.astype(keep.dtype)

            @pl.when(lax.rem(piece, CORES) == core)
            def _():
                keep[users, at] = known
        else:
            at = pl.ds(pl.multiple_of(first, side), side)
            piece = lax.div(first + lax.broadcasted_iota(jnp.int32, known.shape, 1), rows)
            mine = lax.rem(piece, CORES) == core
            keep[users, at] = jnp.where(mine, known, jnp.nan).astype(keep.dtype)
        return carry

    lax.fori_loop(0, counts[0, 0, visit], tile, 0)


def tiles_kernel(first, last, chips, group, groups, close, place, *refs):
    arrived, refs = refs[:chips], refs[chips:]
    (users, peers, rates, peer_rates), refs = refs[:4], refs[4:]
    panel, total = refs[-2:]
    span = chips // groups
    before = 0 if group == 0 else 3 + (chips if last else 0)
    (low, errors, peer_errors), outs = refs[before : before + 3], refs[before + 3 : -2]
    core, chip = place[0], place[1]
    rows = panel.shape[0] // span
    held = total.shape[0]
    mine = slice(group * held, (group + 1) * held)
    if first:
        for k in range(chips):
            origin = lax.rem(chip + chips - k, chips)

            @pl.when(lax.div(origin, span) == group)
            def _():
                at = pl.multiple_of((origin - group * span) * rows, rows)
                panel[pl.ds(at, rows), :] = arrived[k][...].astype(jnp.float32)

    else:
        now = arrived[0][...].astype(jnp.float32)
        for other in arrived[1:]:
            now = now + step_item * other[...].astype(jnp.float32)
        panel[...] = now
    if close:
        low[mine, :] = panel[...].astype(low.dtype)
    else:
        low[mine, :] = jnp.zeros((held, low.shape[1]), low.dtype)
        for j in range(span):
            low[pl.ds(group * held + place_of(close, j, core, rows), rows), :] = panel[
                j * rows : (j + 1) * rows, :
            ].astype(low.dtype)
    for who, known, error in ((users, rates, errors), (peers, peer_rates, peer_errors)):
        for at in range(0, who.shape[0], CHUNK):
            cut = slice(at, at + CHUNK)
            predicted = multiply(who[cut, :], low[mine, :], 1, 1)
            rating = known[cut, mine].astype(jnp.float32)
            error[cut, mine] = jnp.where(rating == rating, rating - predicted, 0.0).astype(error.dtype)
    total[...] = multiply(errors[:, mine], users[...], 0, 0)
    total[...] += multiply(peer_errors[:, mine], peers[...], 0, 0)
    if last:
        for k in range(chips):
            owner = lax.rem(chip + k, chips)

            @pl.when(lax.div(owner, span) == group)
            def _():
                local = owner - group * span
                term = total[pl.ds(place_of(close, local, core, rows), rows), :]
                if k == 0:
                    old = panel[pl.ds(pl.multiple_of(local * rows, rows), rows), :]
                    term = old + step_item * (term - shrinkage * old)
                outs[k][...] = term.astype(outs[k].dtype)

    else:
        for j in range(span):
            cut = slice(j * rows, (j + 1) * rows)
            term = total[pl.ds(place_of(close, j, core, rows), rows), :]
            old = panel[cut, :]
            outs[0][cut, :] = (old + step_item * (term - shrinkage * old)).astype(outs[0].dtype)
            outs[1][cut, :] = term.astype(outs[1].dtype)


def users_kernel(count, *refs):
    (_, low, other_low), refs = refs[:3], refs[3:]
    for i in range(count):
        users, errors, other_errors = refs[3 * i : 3 * i + 3]
        out = refs[3 * count + i]
        for at in range(0, users.shape[0], CHUNK):
            cut = slice(at, at + CHUNK)
            grad = multiply(errors[cut, :], low[...], 1, 0)
            grad = grad + multiply(other_errors[cut, :], other_low[...], 1, 0)
            factor = users[cut, :].astype(jnp.float32)
            out[cut, :] = (factor + step_user * (grad - shrinkage * factor)).astype(out.dtype)


def final_kernel(count, *refs):
    refs = refs[:count] + refs[count + 1 :]
    total = refs[0][...]
    for other in refs[1:count]:
        total = total + step_item * other[...].astype(jnp.float32)
    refs[count][...] = total


def kernel_call(body, name, ins, outs, flops, scratch=(), extra=(), aliases=()):
    return pl.pallas_call(
        body,
        name=name,
        out_shape=tuple(outs),
        in_specs=[SM if x.dtype == jnp.int32 and x.ndim != 6 else VM for x in ins] + [HB] * len(extra),
        out_specs=(VM,) * len(outs),
        scratch_shapes=list(scratch),
        input_output_aliases=dict(aliases),
        compiler_params=pltpu.CompilerParams(vmem_limit_bytes=16 << 20),
        cost_estimate=pl.CostEstimate(flops=flops, bytes_accessed=1024, transcendentals=0),
    )(*ins, *[pltpu.with_memory_space_constraint(x, pltpu.HBM) for x in extra])


def mark_kernel(*refs):
    refs[-1][...] = jnp.zeros_like(refs[-1])


def marked(*arrays):
    return pl.pallas_call(
        mark_kernel,
        name="mark",
        out_shape=pltpu.VMEM((8, 128), jnp.float32),
        in_specs=[VM] * len(arrays),
        out_specs=VM,
        compiler_params=pltpu.CompilerParams(vmem_limit_bytes=16 << 20),
        cost_estimate=pl.CostEstimate(flops=MARK, bytes_accessed=1024, transcendentals=0),
    )(*arrays)


def moved(x, by_strata, by_chip, flip, *, strata, peers):
    pairs = []
    for s in range(strata):
        for h in range(peers):
            chip, core = divmod(h, CORES)
            chip = (chip + by_chip) % (peers // CORES)
            core = 1 - core if flip else core
            pairs.append((s * peers + h, (s + by_strata) % strata * peers + chip * CORES + core))
    return lax.ppermute(x, ("strata", "shard"), pairs)


def shards(user_factors, item_factors, tile_blocks, tile_counts, ratings, mask_words):
    low_type, full_type = jnp.bfloat16, jnp.float32
    strata, peers = lax.axis_size("strata"), lax.axis_size("shard")
    chips = peers // CORES
    move = functools.partial(moved, strata=strata, peers=peers)
    swap = lambda x: move(x, 0, 0, True)
    visits = tile_counts.shape[-1]
    side = ratings.shape[-1]
    rows, width = item_factors.shape
    count = user_factors.shape[0]
    close = rows % side == 0
    held = (chips if close else peers) * rows
    part = chips * rows
    me = lax.axis_index("shard")
    place = jnp.stack([lax.rem(me, CORES), lax.div(me, CORES)]).astype(jnp.int32)
    blocks = jnp.swapaxes(tile_blocks, 3, 4)

    def prepared(visit):
        return kernel_call(
            functools.partial(prepare_kernel, visit, rows, close),
            "prepare",
            [place, *tiles, *other_tiles],
            [pltpu.VMEM((count, held), low_type)] * CORES,
            1024,
        )

    panel_low = item_factors.astype(low_type)
    arrived = [panel_low] + [move(panel_low, 0, k, False) for k in range(1, chips)]
    users, other_users = user_factors, swap(user_factors)
    tiles = [blocks, tile_counts, ratings, mask_words]
    other_tiles = [swap(x) for x in tiles]
    groups = 2 if chips % 2 == 0 else 1
    share, part = held // groups, part // groups
    arrived = [arrived] * groups
    for visit in range(visits):
        last = visit + 1 == visits
        known = prepared(visit)
        shared = [pltpu.VMEM((held, width), low_type)] + [pltpu.VMEM((count, held), low_type)] * 2
        if last:
            shared += [pltpu.VMEM((rows, width), full_type)]
            shared += [pltpu.VMEM((rows, width), low_type)] * (chips - 1)
        made, sent = [], []
        for group in range(groups):
            ins = [place, *arrived[group], users, other_users, *known]
            *outs, = kernel_call(
                functools.partial(tiles_kernel, visit == 0, last, chips, group, groups, close),
                "tiles",
                [*ins, *made],
                shared + ([] if last else [pltpu.VMEM((part, width), low_type)] * 2),
                1024,
                [pltpu.VMEM((part, width), full_type), pltpu.VMEM((share, width), full_type)],
                aliases=[(len(ins) + i, i) for i in range(len(made))],
            )
            made, messages = outs[: len(shared)], outs[len(shared) :]
            if not last:
                sent.append([move(messages[min(k, 1)], 1, k, False) for k in range(chips)])
        low, errors, other_errors, *ends = made
        if last:
            sent = ends[:1] + [move(ends[k], 0, k, False) for k in range(1, chips)]
        arrived = sent
        mark = marked(*sent[LEAD]) if not last else place
        sets = [mark, low, swap(low), users, errors, swap(other_errors)]
        if not last:
            sets += [other_users, other_errors, swap(errors)]
        kind = jax.ShapeDtypeStruct if last else pltpu.VMEM
        users, *other_users = kernel_call(
            functools.partial(users_kernel, 1 if last else 2),
            "users",
            sets,
            [kind((count, width), low_type)] * (1 if last else 2),
            1024,
        )
        if not last:
            other_users = other_users[0]
    (panel,) = kernel_call(
        functools.partial(final_kernel, chips),
        "final",
        arrived,
        [jax.ShapeDtypeStruct((rows, width), full_type)],
        1024,
        extra=[users],
    )
    return (users, panel)


def solution(mesh):
    placed = (
        P(("strata", "shard"), None),
        P(("strata", "shard"), None),
        P("strata", "shard", None, None, None),
        P("strata", "shard", None),
        P("strata", "shard", None, None, None, None),
        P("strata", "shard", None, None, None, None),
    )
    return jax.shard_map(
        shards,
        mesh=mesh,
        in_specs=placed,
        out_specs=(P(("strata", "shard"), None), P(("strata", "shard"), None)),
        check_vma=False,
    )
```

```python
import functools

import jax
import jax.numpy as jnp
from jax import lax
from jax.experimental import pallas as pl
from jax.experimental.pallas import tpu as pltpu
from jax.sharding import PartitionSpec as P

step_user = 0.05
step_item = 0.004
shrinkage = 0.05

VM = pl.BlockSpec(memory_space=pltpu.VMEM)
SM = pl.BlockSpec(memory_space=pltpu.SMEM)
HB = pl.BlockSpec(memory_space=pltpu.HBM)
CORES = 2
CHUNK = 512


def place_of(close, chip, core, rows):
    return pl.multiple_of((chip if close else CORES * chip + core) * rows, rows)


def multiply(a, b, across, over):
    return lax.dot_general(a, b, (((across,), (over,)), ((), ())), preferred_element_type=jnp.float32)


def observed(words):
    count, lanes = words.shape
    shift = lax.broadcasted_iota(jnp.int32, (8, lanes), 0)
    parts = [
        jnp.bitwise_and(jnp.right_shift(jnp.broadcast_to(words[i : i + 1], (8, lanes)), shift), 1)
        for i in range(count)
    ]
    return jnp.concatenate(parts, 0) != 0


def prepare_kernel(visit, rows, close, place, *refs):
    sets = len(refs) // 5
    for i in range(sets):
        lay_out(visit, rows, close, place[0], *refs[4 * i : 4 * i + 4], refs[4 * sets + i])


def lay_out(visit, rows, close, core, blocks, counts, rates, words, keep):
    side = rates.shape[-1]
    nothing = jnp.full((side, side), jnp.nan, keep.dtype)
    for at in range(0, keep.shape[0], side):
        for lane in range(0, keep.shape[1], side):
            keep[at : at + side, lane : lane + side] = nothing

    def tile(k, carry):
        users = pl.ds(pl.multiple_of(blocks[0, 0, visit, 0, k] * side, side), side)
        first = blocks[0, 0, visit, 1, k] * side
        seen = observed(words[0, 0, visit, k])
        known = jnp.where(seen, rates[0, 0, visit, k].astype(jnp.float32), jnp.nan)
        if close:
            piece = lax.div(first, rows)
            at = lax.div(piece, CORES) * rows + lax.rem(first, rows)
            at = pl.ds(pl.multiple_of(at, side), side)
            known = known.astype(keep.dtype)

            @pl.when(lax.rem(piece, CORES) == core)
            def _():
                keep[users, at] = known
        else:
            at = pl.ds(pl.multiple_of(first, side), side)
            piece = lax.div(first + lax.broadcasted_iota(jnp.int32, known.shape, 1), rows)
            mine = lax.rem(piece, CORES) == core
            keep[users, at] = jnp.where(mine, known, jnp.nan).astype(keep.dtype)
        return carry

    lax.fori_loop(0, counts[0, 0, visit], tile, 0)


def tiles_kernel(first, last, chips, groups, close, place, *refs):
    count = chips if first else chips + groups - 1
    arrived, refs = refs[:count], refs[count:]
    (users, peers, rates, peer_rates), refs = refs[:4], refs[4:]
    (low, errors, peer_errors), outs, (panel, total) = refs[:3], refs[3:-2], refs[-2:]
    span = chips // groups
    core, chip = place[0], place[1]
    rows = panel.shape[0] // chips
    if first:
        for k in range(chips):
            origin = lax.rem(chip + chips - k, chips)
            at = pl.multiple_of(origin * rows, rows)
            panel[pl.ds(at, rows), :] = arrived[k][...].astype(jnp.float32)
    else:
        now = arrived[0][...].astype(jnp.float32)
        for other in arrived[1:chips]:
            now = now + step_item * other[...].astype(jnp.float32)
        panel[: span * rows, :] = now
        if groups > 1:
            panel[span * rows :, :] = arrived[chips][...].astype(jnp.float32)
    if close:
        low[...] = panel[...].astype(low.dtype)
    else:
        low[...] = jnp.zeros_like(low)
        for j in range(chips):
            low[pl.ds(place_of(close, j, core, rows), rows), :] = panel[
                j * rows : (j + 1) * rows, :
            ].astype(low.dtype)
    held = low.shape[0]
    for i in range(low.shape[1] // held):
        below = peers.shape[0] + i * held
        peer_errors[below : below + held, :] = low[:, i * held : (i + 1) * held]
    for who, known, error in ((users, rates, errors), (peers, peer_rates, peer_errors)):
        for at in range(0, who.shape[0], CHUNK):
            cut = slice(at, at + CHUNK)
            predicted = multiply(who[cut, :], low[...], 1, 1)
            rating = known[cut, :].astype(jnp.float32)
            error[cut, :] = jnp.where(rating == rating, rating - predicted, 0.0).astype(error.dtype)
    total[...] = multiply(errors[...], users[...], 0, 0)
    total[...] += multiply(peer_errors[: peers.shape[0], :], peers[...], 0, 0)
    if last:
        for k in range(chips):
            owner = lax.rem(chip + k, chips)
            term = total[pl.ds(place_of(close, owner, core, rows), rows), :]
            if k == 0:
                old = panel[pl.ds(pl.multiple_of(owner * rows, rows), rows), :]
                term = old + step_item * (term - shrinkage * old)
            outs[k][...] = term.astype(outs[k].dtype)
    else:
        for j in range(chips):
            joined, plain = outs[2 * (j // span)], outs[2 * (j // span) + 1]
            at, to = slice(j * rows, (j + 1) * rows), slice(j % span * rows, (j % span + 1) * rows)
            term = total[pl.ds(place_of(close, j, core, rows), rows), :]
            old = panel[at, :]
            joined[to, :] = (old + step_item * (term - shrinkage * old)).astype(joined.dtype)
            plain[to, :] = term.astype(plain.dtype)


def users_kernel(last, _, low, *refs):
    if last:
        users, errors, other_errors, out = refs
        sets = [(users, errors, other_errors, out)]
        lows = other_errors
    else:
        users, peers, errors, peer_errors, from_errors, from_peer_errors, out, peer_out = refs
        sets = [(users, errors, from_peer_errors, out), (peers, peer_errors, from_errors, peer_out)]
        lows = from_peer_errors
    held, width = low.shape
    for users, errors, other_errors, out in sets:
        count = users.shape[0]
        for at in range(0, count, CHUNK):
            cut = slice(at, at + CHUNK)
            for lane in range(0, width, held):
                to = slice(lane, lane + held)
                below = pl.ds(count + lane, held)
                grad = multiply(errors[cut, :], low[:, to], 1, 0)
                grad = grad + multiply(other_errors[cut, :], lows[below, :], 1, 0)
                factor = users[cut, to].astype(jnp.float32)
                out[cut, to] = (factor + step_user * (grad - shrinkage * factor)).astype(out.dtype)


def final_kernel(count, *refs):
    refs = refs[:count] + refs[-1:]
    total = refs[0][...]
    for other in refs[1:count]:
        total = total + step_item * other[...].astype(jnp.float32)
    refs[count][...] = total.astype(refs[count].dtype)


def kernel_call(body, name, ins, outs, flops, scratch=(), extra=(), aliases=()):
    return pl.pallas_call(
        body,
        name=name,
        out_shape=tuple(outs),
        in_specs=[SM if x.dtype == jnp.int32 and x.ndim != 6 else VM for x in ins] + [HB] * len(extra),
        out_specs=(VM,) * len(outs),
        scratch_shapes=list(scratch),
        input_output_aliases=dict(aliases),
        compiler_params=pltpu.CompilerParams(vmem_limit_bytes=16 << 20),
        cost_estimate=pl.CostEstimate(flops=flops, bytes_accessed=1024, transcendentals=0),
    )(*ins, *[pltpu.with_memory_space_constraint(x, pltpu.HBM) for x in extra])


def moved(x, by_strata, by_chip, flip, *, strata, peers):
    pairs = []
    for s in range(strata):
        for h in range(peers):
            chip, core = divmod(h, CORES)
            chip = (chip + by_chip) % (peers // CORES)
            core = 1 - core if flip else core
            pairs.append((s * peers + h, (s + by_strata) % strata * peers + chip * CORES + core))
    return lax.ppermute(x, ("strata", "shard"), pairs)


def shards(user_factors, item_factors, tile_blocks, tile_counts, ratings, mask_words):
    low_type, full_type = jnp.bfloat16, jnp.float32
    strata, peers = lax.axis_size("strata"), lax.axis_size("shard")
    chips = peers // CORES
    move = functools.partial(moved, strata=strata, peers=peers)
    swap = lambda x: move(x, 0, 0, True)
    visits = tile_counts.shape[-1]
    side = ratings.shape[-1]
    rows, width = item_factors.shape
    count = user_factors.shape[0]
    close = rows % side == 0
    held = (chips if close else peers) * rows
    part = chips * rows
    me = lax.axis_index("shard")
    place = jnp.stack([lax.rem(me, CORES), lax.div(me, CORES)]).astype(jnp.int32)
    blocks = jnp.swapaxes(tile_blocks, 3, 4)

    def prepared(visit, *sets):
        return kernel_call(
            functools.partial(prepare_kernel, visit, rows, close),
            "prepare",
            [place, *(x for one in sets for x in one)],
            [pltpu.VMEM((count, held), low_type)] * len(sets),
            1024,
        )

    panel_low = item_factors.astype(low_type)
    arrived = [panel_low] + [move(panel_low, 0, k, False) for k in range(1, chips)]
    users, other_users = user_factors, swap(user_factors)
    tiles = [blocks, tile_counts, ratings, mask_words]
    other_tiles = [swap(x) for x in tiles]
    groups = 2 if chips % 2 == 0 else 1
    part = part // groups
    for visit in range(visits):
        last = visit + 1 == visits
        if visit == 0:
            known = [*prepared(visit, tiles), *prepared(visit, other_tiles)]
        else:
            known = prepared(visit, tiles, other_tiles)
        shared = [pltpu.VMEM((held, width), low_type)]
        shared += [pltpu.VMEM((count, held), low_type), pltpu.VMEM((count + width, held), low_type)]
        if last:
            shared += [pltpu.VMEM((rows, width), full_type)]
            shared += [pltpu.VMEM((rows, width), low_type)] * (chips - 1)
        if not last:
            for group in range(groups):
                shared += [pltpu.VMEM((part, width), full_type if group else low_type)]
                shared += [pltpu.VMEM((part, width), low_type)]
        low, errors, other_errors, *ends = kernel_call(
            functools.partial(tiles_kernel, visit == 0, last, chips, groups, close),
            "tiles",
            [place, *arrived, users, other_users, *known],
            shared,
            1024,
            [pltpu.VMEM((chips * rows, width), full_type), pltpu.VMEM((held, width), full_type)],
        )
        if last:
            arrived = ends[:1] + [move(ends[k], 0, k, False) for k in range(1, chips)]
            sets = [place, low, users, errors, swap(other_errors)]
        else:
            if groups > 1:
                others = [move(ends[3], 0, k, False) for k in range(1, chips)]
            arrived = [move(ends[min(k, 1)], 1, k, False) for k in range(chips)]
            if groups > 1:
                (summed,) = kernel_call(
                    functools.partial(final_kernel, chips),
                    "join",
                    [ends[2], *others],
                    [pltpu.VMEM((part, width), low_type)],
                    1024,
                )
                arrived += [move(summed, 1, 0, False)]
            sets = [place, low, users, other_users]
            sets += [errors, other_errors, swap(errors), swap(other_errors)]
        kind = jax.ShapeDtypeStruct if last else pltpu.VMEM
        users, *other_users = kernel_call(
            functools.partial(users_kernel, last),
            "users",
            sets,
            [kind((count, width), low_type)] * (1 if last else 2),
            1024,
        )
        if not last:
            other_users = other_users[0]
    (panel,) = kernel_call(
        functools.partial(final_kernel, chips),
        "final",
        arrived,
        [jax.ShapeDtypeStruct((rows, width), full_type)],
        1024,
        extra=[users],
    )
    return (users, panel)


def solution(mesh):
    placed = (
        P(("strata", "shard"), None),
        P(("strata", "shard"), None),
        P("strata", "shard", None, None, None),
        P("strata", "shard", None),
        P("strata", "shard", None, None, None, None),
        P("strata", "shard", None, None, None, None),
    )
    return jax.shard_map(
        shards,
        mesh=mesh,
        in_specs=placed,
        out_specs=(P(("strata", "shard"), None), P(("strata", "shard"), None)),
        check_vma=False,
    )
```

```python
import functools

import jax
import jax.numpy as jnp
from jax import lax
from jax.experimental import pallas as pl
from jax.experimental.pallas import tpu as pltpu
from jax.sharding import PartitionSpec as P

step_user = 0.05
step_item = 0.004
shrinkage = 0.05

VM = pl.BlockSpec(memory_space=pltpu.VMEM)
SM = pl.BlockSpec(memory_space=pltpu.SMEM)
HB = pl.BlockSpec(memory_space=pltpu.HBM)
CORES = 2
CHUNK = 512
MARK = 1 << 34


def place_of(close, chip, core, rows):
    return pl.multiple_of((chip if close else CORES * chip + core) * rows, rows)


def multiply(a, b, across, over):
    return lax.dot_general(a, b, (((across,), (over,)), ((), ())), preferred_element_type=jnp.float32)


def observed(words):
    count, lanes = words.shape
    shift = lax.broadcasted_iota(jnp.int32, (8, lanes), 0)
    parts = [
        jnp.bitwise_and(jnp.right_shift(jnp.broadcast_to(words[i : i + 1], (8, lanes)), shift), 1)
        for i in range(count)
    ]
    return jnp.concatenate(parts, 0) != 0


def prepare_kernel(visit, rows, close, place, *refs):
    sets = len(refs) // 5
    for i in range(sets):
        lay_out(visit, rows, close, place[0], *refs[4 * i : 4 * i + 4], refs[4 * sets + i])


def lay_out(visit, rows, close, core, blocks, counts, rates, words, keep):
    side = rates.shape[-1]
    nothing = jnp.full((side, side), jnp.nan, keep.dtype)
    for at in range(0, keep.shape[0], side):
        for lane in range(0, keep.shape[1], side):
            keep[at : at + side, lane : lane + side] = nothing

    def tile(k, carry):
        users = pl.ds(pl.multiple_of(blocks[0, 0, visit, 0, k] * side, side), side)
        first = blocks[0, 0, visit, 1, k] * side
        seen = observed(words[0, 0, visit, k])
        known = jnp.where(seen, rates[0, 0, visit, k].astype(jnp.float32), jnp.nan)
        if close:
            piece = lax.div(first, rows)
            at = lax.div(piece, CORES) * rows + lax.rem(first, rows)
            at = pl.ds(pl.multiple_of(at, side), side)
            known = known.astype(keep.dtype)

            @pl.when(lax.rem(piece, CORES) == core)
            def _():
                keep[users, at] = known
        else:
            at = pl.ds(pl.multiple_of(first, side), side)
            piece = lax.div(first + lax.broadcasted_iota(jnp.int32, known.shape, 1), rows)
            mine = lax.rem(piece, CORES) == core
            keep[users, at] = jnp.where(mine, known, jnp.nan).astype(keep.dtype)
        return carry

    lax.fori_loop(0, counts[0, 0, visit], tile, 0)


def tiles_kernel(first, last, chips, groups, close, place, *refs):
    count = chips if first else chips + groups - 1
    arrived, refs = refs[:count], refs[count:]
    (users, peers, rates, peer_rates), refs = refs[:4], refs[4:]
    (low, errors, peer_errors), outs, (panel, total) = refs[:3], refs[3:-2], refs[-2:]
    span = chips // groups
    core, chip = place[0], place[1]
    rows = panel.shape[0] // chips
    if first:
        for k in range(chips):
            origin = lax.rem(chip + chips - k, chips)
            at = pl.multiple_of(origin * rows, rows)
            panel[pl.ds(at, rows), :] = arrived[k][...].astype(jnp.float32)
    else:
        now = arrived[0][...].astype(jnp.float32)
        for other in arrived[1:chips]:
            now = now + step_item * other[...].astype(jnp.float32)
        panel[: span * rows, :] = now
        if groups > 1:
            panel[span * rows :, :] = arrived[chips][...].astype(jnp.float32)
    if close:
        low[...] = panel[...].astype(low.dtype)
    else:
        low[...] = jnp.zeros_like(low)
        for j in range(chips):
            low[pl.ds(place_of(close, j, core, rows), rows), :] = panel[
                j * rows : (j + 1) * rows, :
            ].astype(low.dtype)
    held = low.shape[0]
    for i in range(low.shape[1] // held):
        below = peers.shape[0] + i * held
        peer_errors[below : below + held, :] = low[:, i * held : (i + 1) * held]
    for who, known, error in ((users, rates, errors), (peers, peer_rates, peer_errors)):
        for at in range(0, who.shape[0], CHUNK):
            cut = slice(at, at + CHUNK)
            predicted = multiply(who[cut, :], low[...], 1, 1)
            rating = known[cut, :].astype(jnp.float32)
            error[cut, :] = jnp.where(rating == rating, rating - predicted, 0.0).astype(error.dtype)
    total[...] = multiply(errors[...], users[...], 0, 0)
    total[...] += multiply(peer_errors[: peers.shape[0], :], peers[...], 0, 0)
    if last:
        for k in range(chips):
            owner = lax.rem(chip + k, chips)
            term = total[pl.ds(place_of(close, owner, core, rows), rows), :]
            if k == 0:
                old = panel[pl.ds(pl.multiple_of(owner * rows, rows), rows), :]
                term = old + step_item * (term - shrinkage * old)
            outs[k][...] = term.astype(outs[k].dtype)
    else:
        for j in range(chips):
            joined, plain = outs[2 * (j // span)], outs[2 * (j // span) + 1]
            at, to = slice(j * rows, (j + 1) * rows), slice(j % span * rows, (j % span + 1) * rows)
            term = total[pl.ds(place_of(close, j, core, rows), rows), :]
            old = panel[at, :]
            joined[to, :] = (old + step_item * (term - shrinkage * old)).astype(joined.dtype)
            plain[to, :] = term.astype(plain.dtype)


def users_kernel(last, _, low, *refs):
    if last:
        users, errors, other_errors, out = refs
        sets = [(users, errors, other_errors, out)]
        lows = other_errors
    else:
        users, peers, errors, peer_errors, from_errors, from_peer_errors, out, peer_out = refs
        sets = [(users, errors, from_peer_errors, out), (peers, peer_errors, from_errors, peer_out)]
        lows = from_peer_errors
    held, width = low.shape
    for users, errors, other_errors, out in sets:
        count = users.shape[0]
        for at in range(0, count, CHUNK):
            cut = slice(at, at + CHUNK)
            for lane in range(0, width, held):
                to = slice(lane, lane + held)
                below = pl.ds(count + lane, held)
                grad = multiply(errors[cut, :], low[:, to], 1, 0)
                grad = grad + multiply(other_errors[cut, :], lows[below, :], 1, 0)
                factor = users[cut, to].astype(jnp.float32)
                out[cut, to] = (factor + step_user * (grad - shrinkage * factor)).astype(out.dtype)


def joined(parts):
    total = parts[0][...]
    for other in parts[1:]:
        total = total + step_item * other[...].astype(jnp.float32)
    return total


def join_kernel(count, *refs):
    held, (out, *copies) = refs[count : count + 2], refs[count + 2 :]
    out[...] = joined(refs[:count]).astype(out.dtype)
    for source, copy in zip(held, copies):
        copy[...] = source[...]


def final_kernel(count, *refs):
    refs[-1][...] = joined(refs[:count])


def kernel_call(body, name, ins, outs, flops, scratch=(), extra=()):
    return pl.pallas_call(
        body,
        name=name,
        out_shape=tuple(outs),
        in_specs=[SM if x.dtype == jnp.int32 and x.ndim != 6 else VM for x in ins] + [HB] * len(extra),
        out_specs=(VM,) * len(outs),
        scratch_shapes=list(scratch),
        compiler_params=pltpu.CompilerParams(vmem_limit_bytes=16 << 20),
        cost_estimate=pl.CostEstimate(flops=flops, bytes_accessed=1024, transcendentals=0),
    )(*ins, *[pltpu.with_memory_space_constraint(x, pltpu.HBM) for x in extra])


def mark_kernel(*refs):
    refs[-1][...] = jnp.zeros_like(refs[-1])


def marked(*arrays):
    return pl.pallas_call(
        mark_kernel,
        name="mark",
        out_shape=pltpu.VMEM((8, 128), jnp.float32),
        in_specs=[VM] * len(arrays),
        out_specs=VM,
        compiler_params=pltpu.CompilerParams(vmem_limit_bytes=16 << 20),
        cost_estimate=pl.CostEstimate(flops=MARK, bytes_accessed=1024, transcendentals=0),
    )(*arrays)


def moved(x, by_strata, by_chip, flip, *, strata, peers):
    pairs = []
    for s in range(strata):
        for h in range(peers):
            chip, core = divmod(h, CORES)
            chip = (chip + by_chip) % (peers // CORES)
            core = 1 - core if flip else core
            pairs.append((s * peers + h, (s + by_strata) % strata * peers + chip * CORES + core))
    return lax.ppermute(x, ("strata", "shard"), pairs)


def shards(user_factors, item_factors, tile_blocks, tile_counts, ratings, mask_words):
    low_type, full_type = jnp.bfloat16, jnp.float32
    strata, peers = lax.axis_size("strata"), lax.axis_size("shard")
    chips = peers // CORES
    move = functools.partial(moved, strata=strata, peers=peers)
    swap = lambda x: move(x, 0, 0, True)
    visits = tile_counts.shape[-1]
    side = ratings.shape[-1]
    rows, width = item_factors.shape
    count = user_factors.shape[0]
    close = rows % side == 0
    held = (chips if close else peers) * rows
    part = chips * rows
    me = lax.axis_index("shard")
    place = jnp.stack([lax.rem(me, CORES), lax.div(me, CORES)]).astype(jnp.int32)
    blocks = jnp.swapaxes(tile_blocks, 3, 4)

    def prepared(visit, *sets):
        return kernel_call(
            functools.partial(prepare_kernel, visit, rows, close),
            "prepare",
            [place, *(x for one in sets for x in one)],
            [pltpu.VMEM((count, held), low_type)] * len(sets),
            1024,
        )

    panel_low = item_factors.astype(low_type)
    arrived = [panel_low] + [move(panel_low, 0, k, False) for k in range(1, chips)]
    users, other_users = user_factors, swap(user_factors)
    tiles = [blocks, tile_counts, ratings, mask_words]
    other_tiles = [swap(x) for x in tiles]
    groups = 2 if chips % 2 == 0 else 1
    part = part // groups
    for visit in range(visits):
        last = visit + 1 == visits
        if visit == 0:
            known = [*prepared(visit, tiles), *prepared(visit, other_tiles)]
        else:
            known = prepared(visit, tiles, other_tiles)
        shared = [pltpu.VMEM((held, width), low_type)]
        shared += [pltpu.VMEM((count, held), low_type), pltpu.VMEM((count + width, held), low_type)]
        if last:
            shared += [pltpu.VMEM((rows, width), full_type)]
            shared += [pltpu.VMEM((rows, width), low_type)] * (chips - 1)
        if not last:
            for group in range(groups):
                shared += [pltpu.VMEM((part, width), full_type if group else low_type)]
                shared += [pltpu.VMEM((part, width), low_type)]
        low, errors, other_errors, *ends = kernel_call(
            functools.partial(tiles_kernel, visit == 0, last, chips, groups, close),
            "tiles",
            [place, *arrived, users, other_users, *known],
            shared,
            1024,
            [pltpu.VMEM((chips * rows, width), full_type), pltpu.VMEM((held, width), full_type)],
        )
        if last:
            arrived = ends[:1] + [move(ends[k], 0, k, False) for k in range(1, chips)]
            sets = [place, low, users, errors, swap(other_errors)]
        else:
            if groups > 1:
                others = [move(ends[3], 0, k, False) for k in range(1, chips)]
            arrived = [move(ends[min(k, 1)], 1, k, False) for k in range(chips)]
            if groups > 1:
                summed, errors, other_errors = kernel_call(
                    functools.partial(join_kernel, chips),
                    "join",
                    [ends[2], *others, errors, other_errors],
                    [pltpu.VMEM(x.shape, low_type) for x in (ends[2], errors, other_errors)],
                    1024,
                )
                arrived += [move(summed, 1, 0, False)]
            sets = [marked(arrived[0]), low, users, other_users]
            sets += [errors, other_errors, swap(errors), swap(other_errors)]
        kind = jax.ShapeDtypeStruct if last else pltpu.VMEM
        users, *other_users = kernel_call(
            functools.partial(users_kernel, last),
            "users",
            sets,
            [kind((count, width), low_type)] * (1 if last else 2),
            1024,
        )
        if not last:
            other_users = other_users[0]
    (panel,) = kernel_call(
        functools.partial(final_kernel, chips),
        "final",
        arrived,
        [jax.ShapeDtypeStruct((rows, width), full_type)],
        1024,
        extra=[users],
    )
    return (users, panel)


def solution(mesh):
    placed = (
        P(("strata", "shard"), None),
        P(("strata", "shard"), None),
        P("strata", "shard", None, None, None),
        P("strata", "shard", None),
        P("strata", "shard", None, None, None, None),
        P("strata", "shard", None, None, None, None),
    )
    return jax.shard_map(
        shards,
        mesh=mesh,
        in_specs=placed,
        out_specs=(P(("strata", "shard"), None), P(("strata", "shard"), None)),
        check_vma=False,
    )
```

```python
import functools

import jax
import jax.numpy as jnp
from jax import lax
from jax.experimental import pallas as pl
from jax.experimental.pallas import tpu as pltpu
from jax.sharding import PartitionSpec as P

step_user = 0.05
step_item = 0.004
shrinkage = 0.05

VM = pl.BlockSpec(memory_space=pltpu.VMEM)
SM = pl.BlockSpec(memory_space=pltpu.SMEM)
HB = pl.BlockSpec(memory_space=pltpu.HBM)
CORES = 2
CHUNK = 512
DIRECT = 7
MARK = 1 << 34


def place_of(close, chip, core, rows):
    return pl.multiple_of((chip if close else CORES * chip + core) * rows, rows)


def multiply(a, b, across, over):
    return lax.dot_general(a, b, (((across,), (over,)), ((), ())), preferred_element_type=jnp.float32)


def observed(words):
    count, lanes = words.shape
    shift = lax.broadcasted_iota(jnp.int32, (8, lanes), 0)
    parts = [
        jnp.bitwise_and(jnp.right_shift(jnp.broadcast_to(words[i : i + 1], (8, lanes)), shift), 1)
        for i in range(count)
    ]
    return jnp.concatenate(parts, 0) != 0


def prepare_kernel(visit, rows, close, place, *refs):
    sets = len(refs) // 5
    for i in range(sets):
        lay_out(visit, rows, close, place[0], *refs[4 * i : 4 * i + 4], refs[4 * sets + i])


def lay_out(visit, rows, close, core, blocks, counts, rates, words, keep):
    side = rates.shape[-1]
    nothing = jnp.full((side, side), jnp.nan, keep.dtype)
    for at in range(0, keep.shape[0], side):
        for lane in range(0, keep.shape[1], side):
            keep[at : at + side, lane : lane + side] = nothing

    def tile(k, carry):
        users = pl.ds(pl.multiple_of(blocks[0, 0, visit, 0, k] * side, side), side)
        first = blocks[0, 0, visit, 1, k] * side
        seen = observed(words[0, 0, visit, k])
        known = jnp.where(seen, rates[0, 0, visit, k].astype(jnp.float32), jnp.nan)
        if close:
            piece = lax.div(first, rows)
            at = lax.div(piece, CORES) * rows + lax.rem(first, rows)
            at = pl.ds(pl.multiple_of(at, side), side)
            known = known.astype(keep.dtype)

            @pl.when(lax.rem(piece, CORES) == core)
            def _():
                keep[users, at] = known
        else:
            at = pl.ds(pl.multiple_of(first, side), side)
            piece = lax.div(first + lax.broadcasted_iota(jnp.int32, known.shape, 1), rows)
            mine = lax.rem(piece, CORES) == core
            keep[users, at] = jnp.where(mine, known, jnp.nan).astype(keep.dtype)
        return carry

    lax.fori_loop(0, counts[0, 0, visit], tile, 0)


def tiles_kernel(first, last, chips, direct, close, place, *refs):
    count = chips if first else chips + 1
    arrived, refs = refs[:count], refs[count:]
    (users, peers, rates, peer_rates), refs = refs[:4], refs[4:]
    (low, errors, peer_errors), outs, (panel, total) = refs[:3], refs[3:-2], refs[-2:]
    core, chip = place[0], place[1]
    rows = panel.shape[0] // chips
    if first:
        for k in range(chips):
            origin = lax.rem(chip + chips - k, chips)
            at = pl.multiple_of(origin * rows, rows)
            panel[pl.ds(at, rows), :] = arrived[k][...].astype(jnp.float32)
    else:
        now = arrived[0][...].astype(jnp.float32)
        for other in arrived[1:chips]:
            now = now + step_item * other[...].astype(jnp.float32)
        panel[:direct, :] = now
        panel[direct:, :] = arrived[chips][...].astype(jnp.float32)
    if close:
        low[...] = panel[...].astype(low.dtype)
    else:
        low[...] = jnp.zeros_like(low)
        for j in range(chips):
            low[pl.ds(place_of(close, j, core, rows), rows), :] = panel[
                j * rows : (j + 1) * rows, :
            ].astype(low.dtype)
    held = low.shape[0]
    for i in range(low.shape[1] // held):
        below = peers.shape[0] + i * held
        peer_errors[below : below + held, :] = low[:, i * held : (i + 1) * held]
    for who, known, error in ((users, rates, errors), (peers, peer_rates, peer_errors)):
        for at in range(0, who.shape[0], CHUNK):
            cut = slice(at, at + CHUNK)
            predicted = multiply(who[cut, :], low[...], 1, 1)
            rating = known[cut, :].astype(jnp.float32)
            error[cut, :] = jnp.where(rating == rating, rating - predicted, 0.0).astype(error.dtype)
    total[...] = multiply(errors[...], users[...], 0, 0)
    total[...] += multiply(peer_errors[: peers.shape[0], :], peers[...], 0, 0)
    if last:
        for k in range(chips):
            owner = lax.rem(chip + k, chips)
            term = total[pl.ds(place_of(close, owner, core, rows), rows), :]
            if k == 0:
                old = panel[pl.ds(pl.multiple_of(owner * rows, rows), rows), :]
                term = old + step_item * (term - shrinkage * old)
            outs[k][...] = term.astype(outs[k].dtype)
    else:
        for j in range(chips):
            for (joined, plain), low_end, high_end in (
                (outs[:2], 0, direct),
                (outs[2:], direct, chips * rows),
            ):
                begin, end = max(j * rows, low_end), min((j + 1) * rows, high_end)
                if begin >= end:
                    continue
                at = pl.multiple_of(place_of(close, j, core, rows) + begin - j * rows, 16)
                term = total[pl.ds(at, end - begin), :]
                old = panel[begin:end, :]
                to = slice(begin - low_end, end - low_end)
                joined[to, :] = (old + step_item * (term - shrinkage * old)).astype(joined.dtype)
                plain[to, :] = term.astype(plain.dtype)


def users_kernel(last, _, low, *refs):
    if last:
        users, errors, other_errors, out = refs
        sets = [(users, errors, other_errors, out)]
        lows = other_errors
    else:
        users, peers, errors, peer_errors, from_errors, from_peer_errors, out, peer_out = refs
        sets = [(users, errors, from_peer_errors, out), (peers, peer_errors, from_errors, peer_out)]
        lows = from_peer_errors
    held, width = low.shape
    for users, errors, other_errors, out in sets:
        count = users.shape[0]
        for at in range(0, count, CHUNK):
            cut = slice(at, at + CHUNK)
            for lane in range(0, width, held):
                to = slice(lane, lane + held)
                below = pl.ds(count + lane, held)
                grad = multiply(errors[cut, :], low[:, to], 1, 0)
                grad = grad + multiply(other_errors[cut, :], lows[below, :], 1, 0)
                factor = users[cut, to].astype(jnp.float32)
                out[cut, to] = (factor + step_user * (grad - shrinkage * factor)).astype(out.dtype)


def joined(parts):
    total = parts[0][...]
    for other in parts[1:]:
        total = total + step_item * other[...].astype(jnp.float32)
    return total


def join_kernel(count, *refs):
    held, (out, *copies) = refs[count : count + 2], refs[count + 2 :]
    out[...] = joined(refs[:count]).astype(out.dtype)
    for source, copy in zip(held, copies):
        copy[...] = source[...]


def final_kernel(count, *refs):
    refs[-1][...] = joined(refs[:count])


def kernel_call(body, name, ins, outs, flops, scratch=(), extra=()):
    return pl.pallas_call(
        body,
        name=name,
        out_shape=tuple(outs),
        in_specs=[SM if x.dtype == jnp.int32 and x.ndim != 6 else VM for x in ins] + [HB] * len(extra),
        out_specs=(VM,) * len(outs),
        scratch_shapes=list(scratch),
        compiler_params=pltpu.CompilerParams(vmem_limit_bytes=16 << 20),
        cost_estimate=pl.CostEstimate(flops=flops, bytes_accessed=1024, transcendentals=0),
    )(*ins, *[pltpu.with_memory_space_constraint(x, pltpu.HBM) for x in extra])


def mark_kernel(*refs):
    refs[-1][...] = jnp.zeros_like(refs[-1])


def marked(*arrays):
    return pl.pallas_call(
        mark_kernel,
        name="mark",
        out_shape=pltpu.VMEM((8, 128), jnp.float32),
        in_specs=[VM] * len(arrays),
        out_specs=VM,
        compiler_params=pltpu.CompilerParams(vmem_limit_bytes=16 << 20),
        cost_estimate=pl.CostEstimate(flops=MARK, bytes_accessed=1024, transcendentals=0),
    )(*arrays)


def moved(x, by_strata, by_chip, flip, *, strata, peers):
    pairs = []
    for s in range(strata):
        for h in range(peers):
            chip, core = divmod(h, CORES)
            chip = (chip + by_chip) % (peers // CORES)
            core = 1 - core if flip else core
            pairs.append((s * peers + h, (s + by_strata) % strata * peers + chip * CORES + core))
    return lax.ppermute(x, ("strata", "shard"), pairs)


def shards(user_factors, item_factors, tile_blocks, tile_counts, ratings, mask_words):
    low_type, full_type = jnp.bfloat16, jnp.float32
    strata, peers = lax.axis_size("strata"), lax.axis_size("shard")
    chips = peers // CORES
    move = functools.partial(moved, strata=strata, peers=peers)
    swap = lambda x: move(x, 0, 0, True)
    visits = tile_counts.shape[-1]
    side = ratings.shape[-1]
    rows, width = item_factors.shape
    count = user_factors.shape[0]
    close = rows % side == 0
    held = (chips if close else peers) * rows
    part = chips * rows
    me = lax.axis_index("shard")
    place = jnp.stack([lax.rem(me, CORES), lax.div(me, CORES)]).astype(jnp.int32)
    blocks = jnp.swapaxes(tile_blocks, 3, 4)

    def prepared(visit, *sets):
        return kernel_call(
            functools.partial(prepare_kernel, visit, rows, close),
            "prepare",
            [place, *(x for one in sets for x in one)],
            [pltpu.VMEM((count, held), low_type)] * len(sets),
            1024,
        )

    panel_low = item_factors.astype(low_type)
    arrived = [panel_low] + [move(panel_low, 0, k, False) for k in range(1, chips)]
    users, other_users = user_factors, swap(user_factors)
    tiles = [blocks, tile_counts, ratings, mask_words]
    other_tiles = [swap(x) for x in tiles]
    direct = part * DIRECT // 256 * 16
    for visit in range(visits):
        last = visit + 1 == visits
        if visit == 0:
            known = [*prepared(visit, tiles), *prepared(visit, other_tiles)]
        else:
            known = prepared(visit, tiles, other_tiles)
        shared = [pltpu.VMEM((held, width), low_type)]
        shared += [pltpu.VMEM((count, held), low_type), pltpu.VMEM((count + width, held), low_type)]
        if last:
            shared += [pltpu.VMEM((rows, width), full_type)]
            shared += [pltpu.VMEM((rows, width), low_type)] * (chips - 1)
        else:
            shared += [pltpu.VMEM((direct, width), low_type)] * 2
            shared += [pltpu.VMEM((part - direct, width), kind) for kind in (full_type, low_type)]
        low, errors, other_errors, *ends = kernel_call(
            functools.partial(tiles_kernel, visit == 0, last, chips, direct, close),
            "tiles",
            [place, *arrived, users, other_users, *known],
            shared,
            1024,
            [pltpu.VMEM((chips * rows, width), full_type), pltpu.VMEM((held, width), full_type)],
        )
        if last:
            arrived = ends[:1] + [move(ends[k], 0, k, False) for k in range(1, chips)]
            sets = [place, low, users, errors, swap(other_errors)]
        else:
            others = [move(ends[3], 0, k, False) for k in range(1, chips)]
            arrived = [move(ends[min(k, 1)], 1, k, False) for k in range(chips)]
            summed, errors, other_errors = kernel_call(
                functools.partial(join_kernel, chips),
                "join",
                [ends[2], *others, errors, other_errors],
                [pltpu.VMEM(x.shape, low_type) for x in (ends[2], errors, other_errors)],
                1024,
            )
            arrived += [move(summed, 1, 0, False)]
            sets = [marked(arrived[0]), low, users, other_users]
            sets += [errors, other_errors, swap(errors), swap(other_errors)]
        kind = jax.ShapeDtypeStruct if last else pltpu.VMEM
        users, *other_users = kernel_call(
            functools.partial(users_kernel, last),
            "users",
            sets,
            [kind((count, width), low_type)] * (1 if last else 2),
            1024,
        )
        if not last:
            other_users = other_users[0]
    (panel,) = kernel_call(
        functools.partial(final_kernel, chips),
        "final",
        arrived,
        [jax.ShapeDtypeStruct((rows, width), full_type)],
        1024,
        extra=[users],
    )
    return (users, panel)


def solution(mesh):
    placed = (
        P(("strata", "shard"), None),
        P(("strata", "shard"), None),
        P("strata", "shard", None, None, None),
        P("strata", "shard", None),
        P("strata", "shard", None, None, None, None),
        P("strata", "shard", None, None, None, None),
    )
    return jax.shard_map(
        shards,
        mesh=mesh,
        in_specs=placed,
        out_specs=(P(("strata", "shard"), None), P(("strata", "shard"), None)),
        check_vma=False,
    )
```

```python
import functools

import jax
import jax.numpy as jnp
from jax import lax
from jax.experimental import pallas as pl
from jax.experimental.pallas import tpu as pltpu
from jax.sharding import PartitionSpec as P

step_user = 0.05
step_item = 0.004
shrinkage = 0.05

VM = pl.BlockSpec(memory_space=pltpu.VMEM)
SM = pl.BlockSpec(memory_space=pltpu.SMEM)
HB = pl.BlockSpec(memory_space=pltpu.HBM)
CORES = 2
CHUNK = 512
PASS = 1 << 34
DIRECT = (7, 7)
MARK = 1 << 34


def place_of(close, chip, core, rows):
    return pl.multiple_of((chip if close else CORES * chip + core) * rows, rows)


def multiply(a, b, across, over):
    return lax.dot_general(a, b, (((across,), (over,)), ((), ())), preferred_element_type=jnp.float32)


def observed(words):
    count, lanes = words.shape
    shift = lax.broadcasted_iota(jnp.int32, (8, lanes), 0)
    parts = [
        jnp.bitwise_and(jnp.right_shift(jnp.broadcast_to(words[i : i + 1], (8, lanes)), shift), 1)
        for i in range(count)
    ]
    return jnp.concatenate(parts, 0) != 0


def tables_kernel(blocks, counts, out):
    visits, slots = counts.shape[-1], blocks.shape[-1]
    row = lax.broadcasted_iota(jnp.int32, out.shape, 0)
    lane = lax.broadcasted_iota(jnp.int32, out.shape, 1)
    table = jnp.zeros(out.shape, jnp.int32)
    for t in range(visits):
        entries = [counts[0, 0, t]]
        entries += [blocks[0, 0, t, i, k] for i in range(2) for k in range(slots)]
        for at, entry in enumerate(entries):
            table = jnp.where(jnp.logical_and(row == t, lane == at), entry, table)
    out[...] = table


def prepare_kernel(visit, rows, close, place, *refs):
    sets = len(refs) // 4
    for i in range(sets):
        table, rates, words = refs[3 * i : 3 * i + 3]
        clear(rates.shape[-1], refs[3 * sets + i])
        lay_out(visit, rows, close, place[0], table, rates.at[0, 0, visit], words.at[0, 0, visit], refs[3 * sets + i])


def prepare_first_kernel(rows, close, place, table, rates, words, users, keep, users_here, rates_here, words_here, sem):
    copies = [
        pltpu.make_async_copy(rates.at[0, 0, 0], rates_here, sem.at[0]),
        pltpu.make_async_copy(words.at[0, 0, 0], words_here, sem.at[1]),
        pltpu.make_async_copy(users, users_here, sem.at[2]),
    ]
    for copy in copies:
        copy.start()
    clear(rates.shape[-1], keep)
    for copy in copies[:2]:
        copy.wait()
    lay_out(0, rows, close, place[0], table, rates_here, words_here, keep)
    copies[2].wait()


def clear(side, keep):
    nothing = jnp.full((side, side), jnp.nan, keep.dtype)
    for at in range(0, keep.shape[0], side):
        for lane in range(0, keep.shape[1], side):
            keep[at : at + side, lane : lane + side] = nothing


def lay_out(visit, rows, close, core, table, rates, words, keep):
    slots, side = rates.shape[0], rates.shape[-1]

    def tile(k, carry):
        users = pl.ds(pl.multiple_of(table[visit, 1 + k] * side, side), side)
        first = table[visit, 1 + slots + k] * side
        seen = observed(words[k])
        known = jnp.where(seen, rates[k].astype(jnp.float32), jnp.nan)
        if close:
            piece = lax.div(first, rows)
            at = lax.div(piece, CORES) * rows + lax.rem(first, rows)
            at = pl.ds(pl.multiple_of(at, side), side)

            @pl.when(lax.rem(piece, CORES) == core)
            def _():
                keep[users, at] = known.astype(keep.dtype)

        else:
            at = pl.ds(pl.multiple_of(first, side), side)
            piece = lax.div(first + lax.broadcasted_iota(jnp.int32, known.shape, 1), rows)
            mine = lax.rem(piece, CORES) == core
            keep[users, at] = jnp.where(mine, known, jnp.nan).astype(keep.dtype)
        return carry

    lax.fori_loop(0, table[visit, 0], tile, 0)


def tiles_kernel(first, last, chips, came, direct, close, place, *refs):
    count = chips if first else chips + 1
    arrived, refs = refs[:count], refs[count:]
    (users, peers, rates, peer_rates), refs = refs[:4], refs[4:]
    (low, errors, peer_errors), outs, (panel, total) = refs[:3], refs[3:-2], refs[-2:]
    core, chip = place[0], place[1]
    rows = panel.shape[0] // chips
    if first:
        for k in range(chips):
            origin = lax.rem(chip + chips - k, chips)
            at = pl.multiple_of(origin * rows, rows)
            panel[pl.ds(at, rows), :] = arrived[k][...].astype(jnp.float32)
    else:
        now = arrived[0][...].astype(jnp.float32)
        for other in arrived[1:chips]:
            now = now + step_item * other[...].astype(jnp.float32)
        panel[:came, :] = now
        panel[came:, :] = arrived[chips][...].astype(jnp.float32)
    if close:
        low[...] = panel[...].astype(low.dtype)
    else:
        low[...] = jnp.zeros_like(low)
        for j in range(chips):
            low[pl.ds(place_of(close, j, core, rows), rows), :] = panel[
                j * rows : (j + 1) * rows, :
            ].astype(low.dtype)
    held = low.shape[0]
    for i in range(low.shape[1] // held):
        below = peers.shape[0] + i * held
        peer_errors[below : below + held, :] = low[:, i * held : (i + 1) * held]
    for who, known, error in ((users, rates, errors), (peers, peer_rates, peer_errors)):
        for at in range(0, who.shape[0], CHUNK):
            cut = slice(at, at + CHUNK)
            predicted = multiply(who[cut, :], low[...], 1, 1)
            rating = known[cut, :].astype(jnp.float32)
            error[cut, :] = jnp.where(rating == rating, rating - predicted, 0.0).astype(error.dtype)
    total[...] = multiply(errors[...], users[...], 0, 0)
    total[...] += multiply(peer_errors[: peers.shape[0], :], peers[...], 0, 0)
    if last:
        for k in range(chips):
            owner = lax.rem(chip + k, chips)
            term = total[pl.ds(place_of(close, owner, core, rows), rows), :]
            if k == 0:
                old = panel[pl.ds(pl.multiple_of(owner * rows, rows), rows), :]
                term = old + step_item * (term - shrinkage * old)
            outs[k][...] = term.astype(outs[k].dtype)
    else:
        for j in range(chips):
            for (joined, plain), low_end, high_end in (
                (outs[:2], 0, direct),
                (outs[2:], direct, chips * rows),
            ):
                begin, end = max(j * rows, low_end), min((j + 1) * rows, high_end)
                if begin >= end:
                    continue
                at = pl.multiple_of(place_of(close, j, core, rows) + begin - j * rows, 16)
                term = total[pl.ds(at, end - begin), :]
                old = panel[begin:end, :]
                to = slice(begin - low_end, end - low_end)
                joined[to, :] = (old + step_item * (term - shrinkage * old)).astype(joined.dtype)
                plain[to, :] = term.astype(plain.dtype)


def users_kernel(last, _, low, *refs):
    if last:
        users, errors, other_errors, out = refs
        sets = [(users, errors, other_errors, out)]
        lows = other_errors
    else:
        users, peers, errors, peer_errors, from_errors, from_peer_errors, out, peer_out = refs
        sets = [(users, errors, from_peer_errors, out), (peers, peer_errors, from_errors, peer_out)]
        lows = from_peer_errors
    held, width = low.shape
    for users, errors, other_errors, out in sets:
        count = users.shape[0]
        for at in range(0, count, CHUNK):
            cut = slice(at, at + CHUNK)
            for lane in range(0, width, held):
                to = slice(lane, lane + held)
                below = pl.ds(count + lane, held)
                grad = multiply(errors[cut, :], low[:, to], 1, 0)
                grad = grad + multiply(other_errors[cut, :], lows[below, :], 1, 0)
                factor = users[cut, to].astype(jnp.float32)
                out[cut, to] = (factor + step_user * (grad - shrinkage * factor)).astype(out.dtype)


def joined(parts):
    total = parts[0][...]
    for other in parts[1:]:
        total = total + step_item * other[...].astype(jnp.float32)
    return total


def join_kernel(count, *refs):
    held, (out, *copies) = refs[count : count + 2], refs[count + 2 :]
    out[...] = joined(refs[:count]).astype(out.dtype)
    for source, copy in zip(held, copies):
        copy[...] = source[...]


def final_kernel(count, *refs):
    refs[-1][...] = joined(refs[:count])


def kernel_call(body, name, ins, outs, flops, scratch=(), extra=()):
    return pl.pallas_call(
        body,
        name=name,
        out_shape=tuple(outs),
        in_specs=[SM if x.dtype == jnp.int32 and x.ndim != 6 else VM for x in ins] + [HB] * len(extra),
        out_specs=(VM,) * len(outs),
        scratch_shapes=list(scratch),
        compiler_params=pltpu.CompilerParams(vmem_limit_bytes=16 << 20),
        cost_estimate=pl.CostEstimate(flops=flops, bytes_accessed=1024, transcendentals=0),
    )(*ins, *[pltpu.with_memory_space_constraint(x, pltpu.HBM) for x in extra])


def mark_kernel(*refs):
    refs[-1][...] = jnp.zeros_like(refs[-1])


def pass_kernel(source, _, out):
    out[...] = source[...]


def passed(x, *after):
    return pl.pallas_call(
        pass_kernel,
        name="pass",
        out_shape=pltpu.VMEM(x.shape, x.dtype),
        in_specs=[VM] * 2,
        out_specs=VM,
        compiler_params=pltpu.CompilerParams(vmem_limit_bytes=16 << 20),
        cost_estimate=pl.CostEstimate(flops=PASS, bytes_accessed=1024, transcendentals=0),
    )(x, *after)


def marked(*arrays):
    return pl.pallas_call(
        mark_kernel,
        name="mark",
        out_shape=pltpu.VMEM((8, 128), jnp.float32),
        in_specs=[VM] * len(arrays),
        out_specs=VM,
        compiler_params=pltpu.CompilerParams(vmem_limit_bytes=16 << 20),
        cost_estimate=pl.CostEstimate(flops=MARK, bytes_accessed=1024, transcendentals=0),
    )(*arrays)


def moved(x, by_strata, by_chip, flip, *, strata, peers):
    pairs = []
    for s in range(strata):
        for h in range(peers):
            chip, core = divmod(h, CORES)
            chip = (chip + by_chip) % (peers // CORES)
            core = 1 - core if flip else core
            pairs.append((s * peers + h, (s + by_strata) % strata * peers + chip * CORES + core))
    return lax.ppermute(x, ("strata", "shard"), pairs)


def shards(user_factors, item_factors, tile_blocks, tile_counts, ratings, mask_words):
    low_type, full_type = jnp.bfloat16, jnp.float32
    strata, peers = lax.axis_size("strata"), lax.axis_size("shard")
    chips = peers // CORES
    move = functools.partial(moved, strata=strata, peers=peers)
    swap = lambda x: move(x, 0, 0, True)
    visits = tile_counts.shape[-1]
    side = ratings.shape[-1]
    rows, width = item_factors.shape
    count = user_factors.shape[0]
    close = rows % side == 0
    held = (chips if close else peers) * rows
    part = chips * rows
    me = lax.axis_index("shard")
    place = jnp.stack([lax.rem(me, CORES), lax.div(me, CORES)]).astype(jnp.int32)
    blocks = jnp.swapaxes(tile_blocks, 3, 4)

    def prepared(visit, *sets):
        return kernel_call(
            functools.partial(prepare_kernel, visit, rows, close),
            "prepare",
            [place, *(x for one in sets for x in one)],
            [pltpu.VMEM((count, held), low_type)] * len(sets),
            1024,
        )

    panel_low = item_factors.astype(low_type)
    arrived = [panel_low] + [move(panel_low, 0, k, False) for k in range(1, chips)]
    users, other_users = user_factors, swap(user_factors)
    (table,) = kernel_call(
        tables_kernel,
        "tables",
        [blocks, tile_counts],
        [pltpu.VMEM((8 * -(-visits // 8), 128), jnp.int32)],
        1024,
    )
    tiles = [table, ratings, mask_words]
    other_tiles = [swap(x) for x in tiles]
    direct = 0
    for visit in range(visits):
        last = visit + 1 == visits
        came, direct = direct, part * DIRECT[min(visit, 1)] // 256 * 16
        if visit == 0:
            known, users = pl.pallas_call(
                functools.partial(prepare_first_kernel, rows, close),
                name="prepare",
                out_shape=(pltpu.VMEM((count, held), low_type), pltpu.VMEM(users.shape, users.dtype)),
                in_specs=[SM] * 2 + [HB] * 3,
                out_specs=(VM,) * 2,
                scratch_shapes=[
                    pltpu.VMEM(ratings.shape[3:], ratings.dtype),
                    pltpu.VMEM(mask_words.shape[3:], mask_words.dtype),
                    pltpu.SemaphoreType.DMA((3,)),
                ],
                compiler_params=pltpu.CompilerParams(vmem_limit_bytes=16 << 20),
                cost_estimate=pl.CostEstimate(flops=1024, bytes_accessed=1024, transcendentals=0),
            )(
                place,
                table,
                *[pltpu.with_memory_space_constraint(x, pltpu.HBM) for x in (*tiles[1:], users)],
            )
            known = [known, *prepared(visit, other_tiles)]
            arrived = arrived[:1] + [passed(x, known[1]) for x in arrived[1:]]
        else:
            known = prepared(visit, tiles, other_tiles)
        shared = [pltpu.VMEM((held, width), low_type)]
        shared += [pltpu.VMEM((count, held), low_type), pltpu.VMEM((count + width, held), low_type)]
        if last:
            shared += [pltpu.VMEM((rows, width), full_type)]
            shared += [pltpu.VMEM((rows, width), low_type)] * (chips - 1)
        else:
            shared += [pltpu.VMEM((direct, width), low_type)] * 2
            shared += [pltpu.VMEM((part - direct, width), kind) for kind in (full_type, low_type)]
        low, errors, other_errors, *ends = kernel_call(
            functools.partial(tiles_kernel, visit == 0, last, chips, came, direct, close),
            "tiles",
            [place, *arrived, users, other_users, *known],
            shared,
            1024,
            [pltpu.VMEM((chips * rows, width), full_type), pltpu.VMEM((held, width), full_type)],
        )
        if last:
            arrived = ends[:1] + [move(ends[k], 0, k, False) for k in range(1, chips)]
            sets = [place, low, users, errors, swap(other_errors)]
        else:
            others = [move(ends[3], 0, k, False) for k in range(1, chips)]
            arrived = [move(ends[min(k, 1)], 1, k, False) for k in range(chips)]
            summed, errors, other_errors = kernel_call(
                functools.partial(join_kernel, chips),
                "join",
                [ends[2], *others, errors, other_errors],
                [pltpu.VMEM(x.shape, low_type) for x in (ends[2], errors, other_errors)],
                1024,
            )
            arrived += [move(summed, 1, 0, False)]
            sets = [marked(arrived[0]), low, users, other_users]
            sets += [errors, other_errors, swap(errors), swap(other_errors)]
        kind = jax.ShapeDtypeStruct if last else pltpu.VMEM
        users, *other_users = kernel_call(
            functools.partial(users_kernel, last),
            "users",
            sets,
            [kind((count, width), low_type)] * (1 if last else 2),
            1024,
        )
        if not last:
            other_users = other_users[0]
    (panel,) = kernel_call(
        functools.partial(final_kernel, chips),
        "final",
        arrived,
        [jax.ShapeDtypeStruct((rows, width), full_type)],
        1024,
        extra=[users],
    )
    return (users, panel)


def solution(mesh):
    placed = (
        P(("strata", "shard"), None),
        P(("strata", "shard"), None),
        P("strata", "shard", None, None, None),
        P("strata", "shard", None),
        P("strata", "shard", None, None, None, None),
        P("strata", "shard", None, None, None, None),
    )
    return jax.shard_map(
        shards,
        mesh=mesh,
        in_specs=placed,
        out_specs=(P(("strata", "shard"), None), P(("strata", "shard"), None)),
        check_vma=False,
    )
```

```python
import functools

import jax
import jax.numpy as jnp
from jax import lax
from jax.experimental import pallas as pl
from jax.experimental.pallas import tpu as pltpu
from jax.sharding import PartitionSpec as P

step_user = 0.05
step_item = 0.004
shrinkage = 0.05

VM = pl.BlockSpec(memory_space=pltpu.VMEM)
SM = pl.BlockSpec(memory_space=pltpu.SMEM)
HB = pl.BlockSpec(memory_space=pltpu.HBM)
CORES = 2
CHUNK = 512
PASS = 1 << 34
DIRECT = (7, 7)
MARK = 1 << 34


def place_of(close, chip, core, rows):
    return pl.multiple_of((chip if close else CORES * chip + core) * rows, rows)


def multiply(a, b, across, over):
    return lax.dot_general(a, b, (((across,), (over,)), ((), ())), preferred_element_type=jnp.float32)


def observed(words):
    count, lanes = words.shape
    shift = lax.broadcasted_iota(jnp.int32, (8, lanes), 0)
    parts = [
        jnp.bitwise_and(jnp.right_shift(jnp.broadcast_to(words[i : i + 1], (8, lanes)), shift), 1)
        for i in range(count)
    ]
    return jnp.concatenate(parts, 0) != 0


def tables_kernel(blocks, counts, out):
    visits, slots = counts.shape[-1], blocks.shape[-1]
    row = lax.broadcasted_iota(jnp.int32, out.shape, 0)
    lane = lax.broadcasted_iota(jnp.int32, out.shape, 1)
    table = jnp.zeros(out.shape, jnp.int32)
    for t in range(visits):
        entries = [counts[0, 0, t]]
        entries += [blocks[0, 0, t, i, k] for i in range(2) for k in range(slots)]
        for at, entry in enumerate(entries):
            table = jnp.where(jnp.logical_and(row == t, lane == at), entry, table)
    out[...] = table


def prepare_kernel(visit, rows, close, place, *refs):
    sets = len(refs) // 4
    for i in range(sets):
        table, rates, words = refs[3 * i : 3 * i + 3]
        clear(rates.shape[-1], refs[3 * sets + i])
        lay_out(visit, rows, close, place[0], table, rates.at[0, 0, visit], words.at[0, 0, visit], refs[3 * sets + i])


def prepare_first_kernel(rows, close, place, table, rates, words, users, keep, users_here, rates_here, words_here, sem):
    copies = [
        pltpu.make_async_copy(rates.at[0, 0, 0], rates_here, sem.at[0]),
        pltpu.make_async_copy(words.at[0, 0, 0], words_here, sem.at[1]),
        pltpu.make_async_copy(users, users_here, sem.at[2]),
    ]
    for copy in copies:
        copy.start()
    clear(rates.shape[-1], keep)
    for copy in copies[:2]:
        copy.wait()
    lay_out(0, rows, close, place[0], table, rates_here, words_here, keep)
    copies[2].wait()


def clear(side, keep):
    nothing = jnp.full((side, side), jnp.nan, keep.dtype)
    for at in range(0, keep.shape[0], side):
        for lane in range(0, keep.shape[1], side):
            keep[at : at + side, lane : lane + side] = nothing


def lay_out(visit, rows, close, core, table, rates, words, keep):
    slots, side = rates.shape[0], rates.shape[-1]

    def tile(k, carry):
        users = pl.ds(pl.multiple_of(table[visit, 1 + k] * side, side), side)
        first = table[visit, 1 + slots + k] * side
        seen = observed(words[k])
        known = jnp.where(seen, rates[k].astype(jnp.float32), jnp.nan)
        if close:
            piece = lax.div(first, rows)
            at = lax.div(piece, CORES) * rows + lax.rem(first, rows)
            at = pl.ds(pl.multiple_of(at, side), side)

            @pl.when(lax.rem(piece, CORES) == core)
            def _():
                keep[users, at] = known.astype(keep.dtype)

        else:
            at = pl.ds(pl.multiple_of(first, side), side)
            piece = lax.div(first + lax.broadcasted_iota(jnp.int32, known.shape, 1), rows)
            mine = lax.rem(piece, CORES) == core
            keep[users, at] = jnp.where(mine, known, jnp.nan).astype(keep.dtype)
        return carry

    lax.fori_loop(0, table[visit, 0], tile, 0)


def tiles_kernel(first, last, chips, came, direct, close, place, *refs):
    count = chips if first else chips + 1
    arrived, refs = refs[:count], refs[count:]
    (users, peers, rates, peer_rates), refs = refs[:4], refs[4:]
    (low, errors, peer_errors), outs, (panel, total) = refs[:3], refs[3:-2], refs[-2:]
    core, chip = place[0], place[1]
    rows = panel.shape[0] // chips
    if first:
        for k in range(chips):
            origin = lax.rem(chip + chips - k, chips)
            at = pl.multiple_of(origin * rows, rows)
            panel[pl.ds(at, rows), :] = arrived[k][...].astype(jnp.float32)
    else:
        now = arrived[0][...].astype(jnp.float32)
        for other in arrived[1:chips]:
            now = now + step_item * other[...].astype(jnp.float32)
        panel[:came, :] = now
        panel[came:, :] = arrived[chips][...].astype(jnp.float32)
    if close:
        low[...] = panel[...].astype(low.dtype)
    else:
        low[...] = jnp.zeros_like(low)
        for j in range(chips):
            low[pl.ds(place_of(close, j, core, rows), rows), :] = panel[
                j * rows : (j + 1) * rows, :
            ].astype(low.dtype)
    held = low.shape[0]
    for i in range(low.shape[1] // held):
        below = peers.shape[0] + i * held
        peer_errors[below : below + held, :] = low[:, i * held : (i + 1) * held]
    for who, known, error in ((users, rates, errors), (peers, peer_rates, peer_errors)):
        for at in range(0, who.shape[0], CHUNK):
            cut = slice(at, at + CHUNK)
            predicted = multiply(who[cut, :], low[...], 1, 1)
            rating = known[cut, :].astype(jnp.float32)
            error[cut, :] = jnp.where(rating == rating, rating - predicted, 0.0).astype(error.dtype)
    if last and close:
        for k in range(chips):
            owner = lax.rem(chip + k, chips)
            at = pl.ds(pl.multiple_of(owner * rows, rows), rows)
            if k == 0:
                outs[k][...] = panel[at, :]
            else:
                term = multiply(errors[:, at], users[...], 0, 0)
                term = term + multiply(peer_errors[: peers.shape[0], at], peers[...], 0, 0)
                outs[k][...] = term.astype(outs[k].dtype)
        return
    total[...] = multiply(errors[...], users[...], 0, 0)
    total[...] += multiply(peer_errors[: peers.shape[0], :], peers[...], 0, 0)
    if last:
        for k in range(chips):
            owner = lax.rem(chip + k, chips)
            term = total[pl.ds(place_of(close, owner, core, rows), rows), :]
            if k == 0:
                old = panel[pl.ds(pl.multiple_of(owner * rows, rows), rows), :]
                term = old + step_item * (term - shrinkage * old)
            outs[k][...] = term.astype(outs[k].dtype)
    else:
        for j in range(chips):
            for (joined, plain), low_end, high_end in (
                (outs[:2], 0, direct),
                (outs[2:], direct, chips * rows),
            ):
                begin, end = max(j * rows, low_end), min((j + 1) * rows, high_end)
                if begin >= end:
                    continue
                at = pl.multiple_of(place_of(close, j, core, rows) + begin - j * rows, 16)
                term = total[pl.ds(at, end - begin), :]
                old = panel[begin:end, :]
                to = slice(begin - low_end, end - low_end)
                joined[to, :] = (old + step_item * (term - shrinkage * old)).astype(joined.dtype)
                plain[to, :] = term.astype(plain.dtype)


def own_kernel(place, old, errors, peer_errors, users, peers, out):
    rows = old.shape[0]
    at = pl.ds(pl.multiple_of(place[1] * rows, rows), rows)
    term = multiply(errors[:, at], users[...], 0, 0)
    term = term + multiply(peer_errors[: peers.shape[0], at], peers[...], 0, 0)
    out[...] = old[...] + step_item * (term - shrinkage * old[...])


def users_kernel(last, _, low, *refs):
    if last:
        users, errors, other_errors, out = refs
        sets = [(users, errors, other_errors, out)]
        lows = other_errors
    else:
        users, peers, errors, peer_errors, from_errors, from_peer_errors, out, peer_out = refs
        sets = [(users, errors, from_peer_errors, out), (peers, peer_errors, from_errors, peer_out)]
        lows = from_peer_errors
    held, width = low.shape
    for users, errors, other_errors, out in sets:
        count = users.shape[0]
        for at in range(0, count, CHUNK):
            cut = slice(at, at + CHUNK)
            for lane in range(0, width, held):
                to = slice(lane, lane + held)
                below = pl.ds(count + lane, held)
                grad = multiply(errors[cut, :], low[:, to], 1, 0)
                grad = grad + multiply(other_errors[cut, :], lows[below, :], 1, 0)
                factor = users[cut, to].astype(jnp.float32)
                out[cut, to] = (factor + step_user * (grad - shrinkage * factor)).astype(out.dtype)


def joined(parts):
    total = parts[0][...]
    for other in parts[1:]:
        total = total + step_item * other[...].astype(jnp.float32)
    return total


def join_kernel(count, *refs):
    held, (out, *copies) = refs[count : count + 2], refs[count + 2 :]
    out[...] = joined(refs[:count]).astype(out.dtype)
    for source, copy in zip(held, copies):
        copy[...] = source[...]


def final_kernel(count, *refs):
    refs[-1][...] = joined(refs[:count])


def kernel_call(body, name, ins, outs, flops, scratch=(), extra=()):
    return pl.pallas_call(
        body,
        name=name,
        out_shape=tuple(outs),
        in_specs=[SM if x.dtype == jnp.int32 and x.ndim != 6 else VM for x in ins] + [HB] * len(extra),
        out_specs=(VM,) * len(outs),
        scratch_shapes=list(scratch),
        compiler_params=pltpu.CompilerParams(vmem_limit_bytes=16 << 20),
        cost_estimate=pl.CostEstimate(flops=flops, bytes_accessed=1024, transcendentals=0),
    )(*ins, *[pltpu.with_memory_space_constraint(x, pltpu.HBM) for x in extra])


def mark_kernel(*refs):
    refs[-1][...] = jnp.zeros_like(refs[-1])


def pass_kernel(source, _, out):
    out[...] = source[...]


def passed(x, *after):
    return pl.pallas_call(
        pass_kernel,
        name="pass",
        out_shape=pltpu.VMEM(x.shape, x.dtype),
        in_specs=[VM] * 2,
        out_specs=VM,
        compiler_params=pltpu.CompilerParams(vmem_limit_bytes=16 << 20),
        cost_estimate=pl.CostEstimate(flops=PASS, bytes_accessed=1024, transcendentals=0),
    )(x, *after)


def marked(*arrays):
    return pl.pallas_call(
        mark_kernel,
        name="mark",
        out_shape=pltpu.VMEM((8, 128), jnp.float32),
        in_specs=[VM] * len(arrays),
        out_specs=VM,
        compiler_params=pltpu.CompilerParams(vmem_limit_bytes=16 << 20),
        cost_estimate=pl.CostEstimate(flops=MARK, bytes_accessed=1024, transcendentals=0),
    )(*arrays)


def moved(x, by_strata, by_chip, flip, *, strata, peers):
    pairs = []
    for s in range(strata):
        for h in range(peers):
            chip, core = divmod(h, CORES)
            chip = (chip + by_chip) % (peers // CORES)
            core = 1 - core if flip else core
            pairs.append((s * peers + h, (s + by_strata) % strata * peers + chip * CORES + core))
    return lax.ppermute(x, ("strata", "shard"), pairs)


def shards(user_factors, item_factors, tile_blocks, tile_counts, ratings, mask_words):
    low_type, full_type = jnp.bfloat16, jnp.float32
    strata, peers = lax.axis_size("strata"), lax.axis_size("shard")
    chips = peers // CORES
    move = functools.partial(moved, strata=strata, peers=peers)
    swap = lambda x: move(x, 0, 0, True)
    visits = tile_counts.shape[-1]
    side = ratings.shape[-1]
    rows, width = item_factors.shape
    count = user_factors.shape[0]
    close = rows % side == 0
    held = (chips if close else peers) * rows
    part = chips * rows
    me = lax.axis_index("shard")
    place = jnp.stack([lax.rem(me, CORES), lax.div(me, CORES)]).astype(jnp.int32)
    blocks = jnp.swapaxes(tile_blocks, 3, 4)

    def prepared(visit, *sets):
        return kernel_call(
            functools.partial(prepare_kernel, visit, rows, close),
            "prepare",
            [place, *(x for one in sets for x in one)],
            [pltpu.VMEM((count, held), low_type)] * len(sets),
            1024,
        )

    panel_low = item_factors.astype(low_type)
    arrived = [panel_low] + [move(panel_low, 0, k, False) for k in range(1, chips)]
    users, other_users = user_factors, swap(user_factors)
    (table,) = kernel_call(
        tables_kernel,
        "tables",
        [blocks, tile_counts],
        [pltpu.VMEM((8 * -(-visits // 8), 128), jnp.int32)],
        1024,
    )
    tiles = [table, ratings, mask_words]
    other_tiles = [swap(x) for x in tiles]
    direct = 0
    for visit in range(visits):
        last = visit + 1 == visits
        came, direct = direct, part * DIRECT[min(visit, 1)] // 256 * 16
        if visit == 0:
            known, users = pl.pallas_call(
                functools.partial(prepare_first_kernel, rows, close),
                name="prepare",
                out_shape=(pltpu.VMEM((count, held), low_type), pltpu.VMEM(users.shape, users.dtype)),
                in_specs=[SM] * 2 + [HB] * 3,
                out_specs=(VM,) * 2,
                scratch_shapes=[
                    pltpu.VMEM(ratings.shape[3:], ratings.dtype),
                    pltpu.VMEM(mask_words.shape[3:], mask_words.dtype),
                    pltpu.SemaphoreType.DMA((3,)),
                ],
                compiler_params=pltpu.CompilerParams(vmem_limit_bytes=16 << 20),
                cost_estimate=pl.CostEstimate(flops=1024, bytes_accessed=1024, transcendentals=0),
            )(
                place,
                table,
                *[pltpu.with_memory_space_constraint(x, pltpu.HBM) for x in (*tiles[1:], users)],
            )
            known = [known, *prepared(visit, other_tiles)]
            arrived = arrived[:1] + [passed(x, known[1]) for x in arrived[1:]]
        else:
            known = prepared(visit, tiles, other_tiles)
        shared = [pltpu.VMEM((held, width), low_type)]
        shared += [pltpu.VMEM((count, held), low_type), pltpu.VMEM((count + width, held), low_type)]
        if last:
            shared += [pltpu.VMEM((rows, width), full_type)]
            shared += [pltpu.VMEM((rows, width), low_type)] * (chips - 1)
        else:
            shared += [pltpu.VMEM((direct, width), low_type)] * 2
            shared += [pltpu.VMEM((part - direct, width), kind) for kind in (full_type, low_type)]
        low, errors, other_errors, *ends = kernel_call(
            functools.partial(tiles_kernel, visit == 0, last, chips, came, direct, close),
            "tiles",
            [place, *arrived, users, other_users, *known],
            shared,
            1024,
            [pltpu.VMEM((chips * rows, width), full_type), pltpu.VMEM((held, width), full_type)],
        )
        if last:
            arrived = ends[:1] + [move(ends[k], 0, k, False) for k in range(1, chips)]
            if close:
                arrived[:1] = kernel_call(
                    own_kernel,
                    "own",
                    [place, ends[0], errors, other_errors, users, other_users],
                    [pltpu.VMEM((rows, width), full_type)],
                    1024,
                )
            sets = [place, low, users, errors, swap(other_errors)]
        else:
            others = [move(ends[3], 0, k, False) for k in range(1, chips)]
            arrived = [move(ends[min(k, 1)], 1, k, False) for k in range(chips)]
            summed, errors, other_errors = kernel_call(
                functools.partial(join_kernel, chips),
                "join",
                [ends[2], *others, errors, other_errors],
                [pltpu.VMEM(x.shape, low_type) for x in (ends[2], errors, other_errors)],
                1024,
            )
            arrived += [move(summed, 1, 0, False)]
            sets = [marked(arrived[0]), low, users, other_users]
            sets += [errors, other_errors, swap(errors), swap(other_errors)]
        kind = jax.ShapeDtypeStruct if last else pltpu.VMEM
        users, *other_users = kernel_call(
            functools.partial(users_kernel, last),
            "users",
            sets,
            [kind((count, width), low_type)] * (1 if last else 2),
            1024,
        )
        if not last:
            other_users = other_users[0]
    (panel,) = kernel_call(
        functools.partial(final_kernel, chips),
        "final",
        arrived,
        [jax.ShapeDtypeStruct((rows, width), full_type)],
        1024,
        extra=[users],
    )
    return (users, panel)


def solution(mesh):
    placed = (
        P(("strata", "shard"), None),
        P(("strata", "shard"), None),
        P("strata", "shard", None, None, None),
        P("strata", "shard", None),
        P("strata", "shard", None, None, None, None),
        P("strata", "shard", None, None, None, None),
    )
    return jax.shard_map(
        shards,
        mesh=mesh,
        in_specs=placed,
        out_specs=(P(("strata", "shard"), None), P(("strata", "shard"), None)),
        check_vma=False,
    )
```

```python
import functools

import jax
import jax.numpy as jnp
from jax import lax
from jax.experimental import pallas as pl
from jax.experimental.pallas import tpu as pltpu
from jax.sharding import PartitionSpec as P

step_user = 0.05
step_item = 0.004
shrinkage = 0.05

VM = pl.BlockSpec(memory_space=pltpu.VMEM)
SM = pl.BlockSpec(memory_space=pltpu.SMEM)
HB = pl.BlockSpec(memory_space=pltpu.HBM)
CORES = 2
CHUNK = 512
PASS = 1 << 34
DIRECT = (7, 7)
MARK = 1 << 34


def place_of(close, chip, core, rows):
    return pl.multiple_of((chip if close else CORES * chip + core) * rows, rows)


def multiply(a, b, across, over):
    return lax.dot_general(a, b, (((across,), (over,)), ((), ())), preferred_element_type=jnp.float32)


def observed(words):
    count, lanes = words.shape
    shift = lax.broadcasted_iota(jnp.int32, (8, lanes), 0)
    parts = [
        jnp.bitwise_and(jnp.right_shift(jnp.broadcast_to(words[i : i + 1], (8, lanes)), shift), 1)
        for i in range(count)
    ]
    return jnp.concatenate(parts, 0) != 0


def tables_kernel(blocks, counts, out):
    visits, slots = counts.shape[-1], blocks.shape[-1]
    row = lax.broadcasted_iota(jnp.int32, out.shape, 0)
    lane = lax.broadcasted_iota(jnp.int32, out.shape, 1)
    table = jnp.zeros(out.shape, jnp.int32)
    for t in range(visits):
        entries = [counts[0, 0, t]]
        entries += [blocks[0, 0, t, i, k] for i in range(2) for k in range(slots)]
        for at, entry in enumerate(entries):
            table = jnp.where(jnp.logical_and(row == t, lane == at), entry, table)
    out[...] = table


def prepare_kernel(visit, rows, close, place, *refs):
    sets = len(refs) // 4
    for i in range(sets):
        table, rates, words = refs[3 * i : 3 * i + 3]
        clear(rates.shape[-1], refs[3 * sets + i])
        lay_out(visit, rows, close, place[0], table, rates.at[0, 0, visit], words.at[0, 0, visit], refs[3 * sets + i])


def prepare_first_kernel(rows, close, place, table, rates, words, users, keep, users_here, rates_here, words_here, sem):
    copies = [
        pltpu.make_async_copy(rates.at[0, 0, 0], rates_here, sem.at[0]),
        pltpu.make_async_copy(words.at[0, 0, 0], words_here, sem.at[1]),
        pltpu.make_async_copy(users, users_here, sem.at[2]),
    ]
    for copy in copies:
        copy.start()
    clear(rates.shape[-1], keep)
    for copy in copies[:2]:
        copy.wait()
    lay_out(0, rows, close, place[0], table, rates_here, words_here, keep)
    copies[2].wait()


def clear(side, keep):
    nothing = jnp.full((side, side), jnp.nan, keep.dtype)
    for at in range(0, keep.shape[0], side):
        for lane in range(0, keep.shape[1], side):
            keep[at : at + side, lane : lane + side] = nothing


def lay_out(visit, rows, close, core, table, rates, words, keep):
    slots, side = rates.shape[0], rates.shape[-1]

    def tile(k, carry):
        users = pl.ds(pl.multiple_of(table[visit, 1 + k] * side, side), side)
        first = table[visit, 1 + slots + k] * side
        seen = observed(words[k])
        known = jnp.where(seen, rates[k].astype(jnp.float32), jnp.nan)
        if close:
            piece = lax.div(first, rows)
            at = lax.div(piece, CORES) * rows + lax.rem(first, rows)
            at = pl.ds(pl.multiple_of(at, side), side)

            @pl.when(lax.rem(piece, CORES) == core)
            def _():
                keep[users, at] = known.astype(keep.dtype)

        else:
            at = pl.ds(pl.multiple_of(first, side), side)
            piece = lax.div(first + lax.broadcasted_iota(jnp.int32, known.shape, 1), rows)
            mine = lax.rem(piece, CORES) == core
            keep[users, at] = jnp.where(mine, known, jnp.nan).astype(keep.dtype)
        return carry

    lax.fori_loop(0, table[visit, 0], tile, 0)


def tiles_kernel(first, last, chips, came, direct, close, place, *refs):
    count = chips if first else chips + 1
    arrived, refs = refs[:count], refs[count:]
    (users, peers, rates, peer_rates), refs = refs[:4], refs[4:]
    (low, errors, peer_errors), outs, (panel, total) = refs[:3], refs[3:-2], refs[-2:]
    core, chip = place[0], place[1]
    rows = panel.shape[0] // chips
    if first:
        for k in range(chips):
            origin = lax.rem(chip + chips - k, chips)
            at = pl.multiple_of(origin * rows, rows)
            panel[pl.ds(at, rows), :] = arrived[k][...].astype(jnp.float32)
    else:
        now = arrived[0][...].astype(jnp.float32)
        for other in arrived[1:chips]:
            now = now + step_item * other[...].astype(jnp.float32)
        panel[:came, :] = now
        panel[came:, :] = arrived[chips][...].astype(jnp.float32)
    if close:
        low[...] = panel[...].astype(low.dtype)
    else:
        low[...] = jnp.zeros_like(low)
        for j in range(chips):
            low[pl.ds(place_of(close, j, core, rows), rows), :] = panel[
                j * rows : (j + 1) * rows, :
            ].astype(low.dtype)
    held = low.shape[0]
    for i in range(low.shape[1] // held):
        below = peers.shape[0] + i * held
        peer_errors[below : below + held, :] = low[:, i * held : (i + 1) * held]
    for who, known, error in ((users, rates, errors), (peers, peer_rates, peer_errors)):
        for at in range(0, who.shape[0], CHUNK):
            cut = slice(at, at + CHUNK)
            predicted = multiply(who[cut, :], low[...], 1, 1)
            rating = known[cut, :].astype(jnp.float32)
            error[cut, :] = jnp.where(rating == rating, rating - predicted, 0.0).astype(error.dtype)
    if last and close:
        for k in range(chips):
            owner = lax.rem(chip + k, chips)
            at = pl.ds(pl.multiple_of(owner * rows, rows), rows)
            if k == 0:
                outs[k][...] = panel[at, :]
            else:
                term = multiply(errors[:, at], users[...], 0, 0)
                term = term + multiply(peer_errors[: peers.shape[0], at], peers[...], 0, 0)
                outs[k][...] = term.astype(outs[k].dtype)
        return
    total[...] = multiply(errors[...], users[...], 0, 0)
    total[...] += multiply(peer_errors[: peers.shape[0], :], peers[...], 0, 0)
    if last:
        for k in range(chips):
            owner = lax.rem(chip + k, chips)
            term = total[pl.ds(place_of(close, owner, core, rows), rows), :]
            if k == 0:
                old = panel[pl.ds(pl.multiple_of(owner * rows, rows), rows), :]
                term = old + step_item * (term - shrinkage * old)
            outs[k][...] = term.astype(outs[k].dtype)
    else:
        for j in range(chips):
            for (joined, plain), low_end, high_end in (
                (outs[:2], 0, direct),
                (outs[2:], direct, chips * rows),
            ):
                begin, end = max(j * rows, low_end), min((j + 1) * rows, high_end)
                if begin >= end:
                    continue
                at = pl.multiple_of(place_of(close, j, core, rows) + begin - j * rows, 16)
                term = total[pl.ds(at, end - begin), :]
                old = panel[begin:end, :]
                to = slice(begin - low_end, end - low_end)
                joined[to, :] = (old + step_item * (term - shrinkage * old)).astype(joined.dtype)
                plain[to, :] = term.astype(plain.dtype)


def own_kernel(place, old, errors, peer_errors, users, peers, out):
    rows = old.shape[0]
    at = pl.ds(pl.multiple_of(place[1] * rows, rows), rows)
    term = multiply(errors[:, at], users[...], 0, 0)
    term = term + multiply(peer_errors[: peers.shape[0], at], peers[...], 0, 0)
    out[...] = old[...] + step_item * (term - shrinkage * old[...])


def users_kernel(last, _, low, *refs):
    if last:
        users, errors, other_errors, out = refs
        sets = [(users, errors, other_errors, out)]
        lows = other_errors
    else:
        users, peers, errors, peer_errors, from_errors, from_peer_errors, out, peer_out = refs
        sets = [(users, errors, from_peer_errors, out), (peers, peer_errors, from_errors, peer_out)]
        lows = from_peer_errors
    held, width = low.shape
    for users, errors, other_errors, out in sets:
        count = users.shape[0]
        for at in range(0, count, CHUNK):
            cut = slice(at, at + CHUNK)
            for lane in range(0, width, held):
                to = slice(lane, lane + held)
                below = pl.ds(count + lane, held)
                grad = multiply(errors[cut, :], low[:, to], 1, 0)
                grad = grad + multiply(other_errors[cut, :], lows[below, :], 1, 0)
                factor = users[cut, to].astype(jnp.float32)
                out[cut, to] = (factor + step_user * (grad - shrinkage * factor)).astype(out.dtype)


def joined(parts):
    total = parts[0][...]
    for other in parts[1:]:
        total = total + step_item * other[...].astype(jnp.float32)
    return total


def join_kernel(count, *refs):
    held, (out, *copies) = refs[count : count + 2], refs[count + 2 :]
    out[...] = joined(refs[:count]).astype(out.dtype)
    for source, copy in zip(held, copies):
        copy[...] = source[...]


def final_kernel(count, *refs):
    refs[-1][...] = joined(refs[:count])


def kernel_call(body, name, ins, outs, flops, scratch=(), extra=()):
    return pl.pallas_call(
        body,
        name=name,
        out_shape=tuple(outs),
        in_specs=[SM if x.dtype == jnp.int32 and x.ndim != 6 else VM for x in ins] + [HB] * len(extra),
        out_specs=(VM,) * len(outs),
        scratch_shapes=list(scratch),
        compiler_params=pltpu.CompilerParams(vmem_limit_bytes=16 << 20),
        cost_estimate=pl.CostEstimate(flops=flops, bytes_accessed=1024, transcendentals=0),
    )(*ins, *[pltpu.with_memory_space_constraint(x, pltpu.HBM) for x in extra])


def mark_kernel(*refs):
    refs[-1][...] = jnp.zeros_like(refs[-1])


def pass_kernel(source, _, out):
    out[...] = source[...]


def passed(x, *after):
    return pl.pallas_call(
        pass_kernel,
        name="pass",
        out_shape=pltpu.VMEM(x.shape, x.dtype),
        in_specs=[VM] * 2,
        out_specs=VM,
        compiler_params=pltpu.CompilerParams(vmem_limit_bytes=16 << 20),
        cost_estimate=pl.CostEstimate(flops=PASS, bytes_accessed=1024, transcendentals=0),
    )(x, *after)


def marked(*arrays):
    return pl.pallas_call(
        mark_kernel,
        name="mark",
        out_shape=pltpu.VMEM((8, 128), jnp.float32),
        in_specs=[VM] * len(arrays),
        out_specs=VM,
        compiler_params=pltpu.CompilerParams(vmem_limit_bytes=16 << 20),
        cost_estimate=pl.CostEstimate(flops=MARK, bytes_accessed=1024, transcendentals=0),
    )(*arrays)


def moved(x, by_strata, by_chip, flip, *, strata, peers):
    pairs = []
    for s in range(strata):
        for h in range(peers):
            chip, core = divmod(h, CORES)
            chip = (chip + by_chip) % (peers // CORES)
            core = 1 - core if flip else core
            pairs.append((s * peers + h, (s + by_strata) % strata * peers + chip * CORES + core))
    return lax.ppermute(x, ("strata", "shard"), pairs)


def shards(user_factors, item_factors, tile_blocks, tile_counts, ratings, mask_words):
    low_type, full_type = jnp.bfloat16, jnp.float32
    strata, peers = lax.axis_size("strata"), lax.axis_size("shard")
    chips = peers // CORES
    move = functools.partial(moved, strata=strata, peers=peers)
    swap = lambda x: move(x, 0, 0, True)
    visits = tile_counts.shape[-1]
    side = ratings.shape[-1]
    rows, width = item_factors.shape
    count = user_factors.shape[0]
    close = rows % side == 0
    held = (chips if close else peers) * rows
    part = chips * rows
    me = lax.axis_index("shard")
    place = jnp.stack([lax.rem(me, CORES), lax.div(me, CORES)]).astype(jnp.int32)
    blocks = jnp.swapaxes(tile_blocks, 3, 4)

    def prepared(visit, *sets):
        return kernel_call(
            functools.partial(prepare_kernel, visit, rows, close),
            "prepare",
            [place, *(x for one in sets for x in one)],
            [pltpu.VMEM((count, held), low_type)] * len(sets),
            1024,
        )

    panel_low = item_factors.astype(low_type)
    arrived = [panel_low] + [move(panel_low, 0, k, False) for k in range(1, chips)]
    users, other_users = user_factors, swap(user_factors)
    (table,) = kernel_call(
        tables_kernel,
        "tables",
        [blocks, tile_counts],
        [pltpu.VMEM((8 * -(-visits // 8), 128), jnp.int32)],
        1024,
    )
    tiles = [table, ratings, mask_words]
    other_tiles = [swap(x) for x in tiles]
    direct = 0
    for visit in range(visits):
        last = visit + 1 == visits
        came, direct = direct, part * DIRECT[min(visit, 1)] // 256 * 16
        if visit == 0:
            known, users = pl.pallas_call(
                functools.partial(prepare_first_kernel, rows, close),
                name="prepare",
                out_shape=(pltpu.VMEM((count, held), low_type), pltpu.VMEM(users.shape, users.dtype)),
                in_specs=[SM] * 2 + [HB] * 3,
                out_specs=(VM,) * 2,
                scratch_shapes=[
                    pltpu.VMEM(ratings.shape[3:], ratings.dtype),
                    pltpu.VMEM(mask_words.shape[3:], mask_words.dtype),
                    pltpu.SemaphoreType.DMA((3,)),
                ],
                compiler_params=pltpu.CompilerParams(vmem_limit_bytes=16 << 20),
                cost_estimate=pl.CostEstimate(flops=1024, bytes_accessed=1024, transcendentals=0),
            )(
                place,
                table,
                *[pltpu.with_memory_space_constraint(x, pltpu.HBM) for x in (*tiles[1:], users)],
            )
            known = [known, *prepared(visit, other_tiles)]
            arrived = arrived[:1] + [passed(x, known[1]) for x in arrived[1:]]
        else:
            known = prepared(visit, tiles, other_tiles)
        shared = [pltpu.VMEM((held, width), low_type)]
        shared += [pltpu.VMEM((count, held), low_type), pltpu.VMEM((count + width, held), low_type)]
        if last:
            shared += [pltpu.VMEM((rows, width), full_type)]
            shared += [pltpu.VMEM((rows, width), low_type)] * (chips - 1)
        else:
            shared += [pltpu.VMEM((direct, width), low_type)] * 2
            shared += [pltpu.VMEM((part - direct, width), kind) for kind in (full_type, low_type)]
        low, errors, other_errors, *ends = kernel_call(
            functools.partial(tiles_kernel, visit == 0, last, chips, came, direct, close),
            "tiles",
            [place, *arrived, users, other_users, *known],
            shared,
            1024,
            [pltpu.VMEM((chips * rows, width), full_type), pltpu.VMEM((held, width), full_type)],
        )
        if last:
            arrived = ends[:1] + [move(ends[k], 0, k, False) for k in range(1, chips)]
            if close:
                arrived[:1] = kernel_call(
                    own_kernel,
                    "own",
                    [place, ends[0], errors, other_errors, users, other_users],
                    [pltpu.VMEM((rows, width), full_type)],
                    1024,
                )
            sets = [place, low, users, errors, swap(other_errors)]
        else:
            others = [move(ends[3], 0, k, False) for k in range(1, chips)]
            arrived = [move(ends[min(k, 1)], 1, k, False) for k in range(chips)]
            summed, errors, other_errors = kernel_call(
                functools.partial(join_kernel, chips),
                "join",
                [ends[2], *others, errors, other_errors],
                [pltpu.VMEM(x.shape, low_type) for x in (ends[2], errors, other_errors)],
                1024,
            )
            arrived += [move(summed, 1, 0, False)]
            sets = [marked(*arrived[:2]), low, users, other_users]
            sets += [errors, other_errors, swap(errors), swap(other_errors)]
        kind = jax.ShapeDtypeStruct if last else pltpu.VMEM
        users, *other_users = kernel_call(
            functools.partial(users_kernel, last),
            "users",
            sets,
            [kind((count, width), low_type)] * (1 if last else 2),
            1024,
        )
        if not last:
            other_users = other_users[0]
    (panel,) = kernel_call(
        functools.partial(final_kernel, chips),
        "final",
        arrived,
        [jax.ShapeDtypeStruct((rows, width), full_type)],
        1024,
        extra=[users],
    )
    return (users, panel)


def solution(mesh):
    placed = (
        P(("strata", "shard"), None),
        P(("strata", "shard"), None),
        P("strata", "shard", None, None, None),
        P("strata", "shard", None),
        P("strata", "shard", None, None, None, None),
        P("strata", "shard", None, None, None, None),
    )
    return jax.shard_map(
        shards,
        mesh=mesh,
        in_specs=placed,
        out_specs=(P(("strata", "shard"), None), P(("strata", "shard"), None)),
        check_vma=False,
    )
```
